128 devices in a mesh: replica: 4 (over y_lo, core), fsdp: 32 (over z, x, y_hi).
Axes of the slice: x: 4, y: 4 (y_hi: 2, y_lo: 2; y = y_hi * 2 + y_lo), z: 4, core: 2. Of those that a mesh axis runs over, the one named last changes fastest.
Arguments:
- inputs: bfloat16 [4, 4096, 4096], P('replica', 'fsdp'), may hold values from -6 to 6
- segments: int32 [4, 4096], P('replica', 'fsdp'), may hold values from 0 to 15, never falling along the last dimension, each value on 1 to 512 neighbouring positions
- cotangent: bfloat16 [4, 4096, 14336], P('replica', None, 'fsdp'), may hold values from -6 to 6
- base: float32 [4096, 14336], P('replica', 'fsdp'), may hold values from -6 to 6
- momentum: float32 [4096, 14336], P('replica', 'fsdp'), may hold values from -2 to 2
Outputs:
- new_base: float32 [4096, 14336], P('replica', 'fsdp')
- new_momentum: float32 [4096, 14336], P('replica', 'fsdp')
- weights: bfloat16 [4096, 14336], P(None, 'fsdp')
The draws below stay inside these ranges and needn't reach their ends.
All inputs are finite; a program needn't handle non-finite values. Where the reference program divides by a largest or mean magnitude, that divisor is 1e-20 or more.
Results may differ from the reference program's by a relative error of at most 0.0095.
Values may be sent and summed in bfloat16 or wider, within the bound.
A program may use at most 128 MiB of HBM per device.

```python
import math
import jax
import jax.numpy as jnp
import numpy as np
from jax import lax

D = 4096
FF = 14336
BLOCK = 128
DOCS = 16
TOK_G = 4096
REPLICAS = 4


def levels(own_key, dims, cuts, smallest, largest):
    factor_of, own = 1.0, jax.random.fold_in(own_key, 6)
    for dim, parts in cuts:
        draws = jnp.exp(jax.random.uniform(jax.random.fold_in(own, dim), (parts,), jnp.float32, smallest / len(cuts), largest / len(cuts)))
        factor_of = factor_of * jnp.repeat(draws, dims[dim] // parts).reshape([-1 if axis == dim else 1 for axis in range(len(dims))])
    return factor_of


def length_profile(count, total, most, skew):
    portions = [(1 << 20) // math.isqrt(grade ** skew) + 1 for grade in range(2, count + 1)]
    rest, holding = total - most - (count - 1), [1] * (count - 1)
    while rest > 0:
        movable = [i for i in range(count - 1) if holding[i] < most]
        pool, remaining = sum([portions[i] for i in movable]), rest
        for i in movable:
            addition = min(most - holding[i], max(1, remaining * portions[i] // pool), rest)
            holding[i] = holding[i] + addition
            rest = rest - addition
    return np.array([most] + holding)


def uneven_parts(own_key, amount, total, limit, lean):
    if amount == 2:
        one = jax.random.randint(own_key, (), max(1, total - limit), min(limit, total - 1) + 1)
        return jnp.stack([one, total - one])
    tallies = jnp.asarray(length_profile(amount, total, limit, lean), jnp.int32)
    twos = (amount - 1) // 2
    source_of, receiver = tallies[1:1 + 2 * twos:2], tallies[2:2 + 2 * twos:2]
    margin = jnp.minimum(source_of - 1, limit - receiver)
    moved = jax.random.randint(jax.random.fold_in(own_key, 1), (twos,), 0, 1 << 20) % (margin + 1)
    tallies = tallies.at[1:1 + 2 * twos:2].set(source_of - moved).at[2:2 + 2 * twos:2].set(receiver + moved)
    return tallies[jax.random.permutation(jax.random.fold_in(own_key, 2), amount)]


def normal_values(key, dims, deviation, reach, pieces=(), held_as=jnp.bfloat16):
    level = levels(key, dims, pieces, -0.22, 0.18) if pieces else 1.0
    drawn = jax.random.normal(key, dims, jnp.float32) * deviation * level
    return jnp.minimum(jnp.maximum(drawn, -reach), reach).astype(held_as)


def setup_inputs(seed: int = 0) -> dict:
    streams_of = jax.random.split(jax.random.key(seed), 6)
    inputs = normal_values(streams_of[0], (REPLICAS, TOK_G, D), 1.0, 6.0, ((0, 4), (1, 32)))
    segments = jax.vmap(lambda own: jnp.searchsorted(jnp.cumsum(uneven_parts(own, DOCS, TOK_G, 2 * TOK_G // DOCS, 2)), jnp.arange(TOK_G), side="right"))(jax.random.split(streams_of[1], REPLICAS)).reshape((REPLICAS, TOK_G)).astype(jnp.int32)
    cotangent = normal_values(streams_of[2], (REPLICAS, TOK_G, FF), 1.0, 6.0, ((0, 4), (2, 32)))
    base = normal_values(streams_of[3], (D, FF), 1.0, 6.0, ((0, 4), (1, 32)), jnp.float32)
    momentum = normal_values(streams_of[4], (D, FF), 0.3, 2.0, ((0, 4), (1, 32)), jnp.float32)
    return dict(inputs=inputs, segments=segments, cotangent=cotangent, base=base, momentum=momentum)


inner_rate = 2.0
outer_rate = 0.7
nesterov_coef = 0.9
epsilon = 1e-6


def reference(inputs, segments, cotangent, base, momentum):
    total = jnp.zeros((D, FF), jnp.float32)
    for group in range(REPLICAS):
        onehot = (segments[group][:, None] == jnp.arange(DOCS, dtype=jnp.int32)[None, :]).astype(jnp.float32)
        count = jnp.sum(onehot, axis=0)
        tok_weight = jnp.dot(onehot, 1.0 / count, precision=lax.Precision.HIGHEST)
        weighted = (inputs[group].astype(jnp.float32) * tok_weight[:, None]).astype(jnp.bfloat16)
        grad = lax.dot_general(weighted, cotangent[group], (((0,), (0,)), ((), ())), preferred_element_type=jnp.float32)
        outer = inner_rate * grad
        blocks = outer.reshape(D // BLOCK, BLOCK, FF)
        scale = (jnp.max(jnp.abs(blocks), axis=1) + epsilon).astype(jnp.bfloat16)
        coded = (blocks / scale[:, None, :].astype(jnp.float32)).astype(jnp.bfloat16)
        decoded = coded.astype(jnp.float32) * scale[:, None, :].astype(jnp.float32)
        total = total + decoded.reshape(D, FF)
    average = total / REPLICAS
    new_momentum = nesterov_coef * momentum + average
    new_base = base - outer_rate * (average + nesterov_coef * new_momentum)
    return new_base, new_momentum, new_base.astype(jnp.bfloat16)
```

```python
import jax
import jax.numpy as jnp
from jax import lax
from jax.experimental import pallas as pl
from jax.experimental.pallas import tpu as pltpu
from jax.sharding import PartitionSpec as P

D = 4096
BLOCK = 128
DOCS = 16
STEPS = 8
SIDE = 4
TOK = 128
COLS = 448
HALF = D // 2
OWN = D // 4
EARLY = 3

inner_rate = 2.0
outer_rate = 0.7
nesterov_coef = 0.9
epsilon = 1e-06
MESH = pl.DeviceIdType.MESH


def kernel(
    seg_ref, inp_ref, cot_ref, base_ref, mom_ref,
    nb_out, nm_out, w_out,
    xin, xa, xb, ysend, cot, base, mom, acc, keep, xs, xr, ps, rr, wt, cnt,
    load_sem, cot_sem, cnt_send, cnt_recv,
    a1s, a1r, a2s, a2r, b1s, b1r, b2s, b2r, ys, yr, cots, cotr,
    xss, xsr, pss, psr, wcs, wcr, wls, wlr, wfs, wfr, out_sem,
):
    rep, f = lax.axis_index("replica"), lax.axis_index("fsdp")
    lo, core = rep // 2, rep % 2
    z, x, h = f // 8, (f // 2) % 4, f % 2

    def dev(x_=x, z_=z, h_=h, lo_=lo, core_=core):
        return (lo_ * 2 + core_, z_ * 8 + x_ * 2 + h_)

    def rot(v, d):
        return lax.rem(v + d, SIDE)

    other_core = dev(core_=1 - core)
    other_lo = dev(lo_=1 - lo)
    other_h = dev(h_=1 - h)

    def remote(src, dst, ss, rs, to):
        return pltpu.make_async_remote_copy(
            src_ref=src, dst_ref=dst, send_sem=ss, recv_sem=rs, device_id=to, device_id_type=MESH
        )

    load_in = pltpu.make_async_copy(inp_ref, xin, load_sem.at[0])
    load_base = pltpu.make_async_copy(base_ref, base, load_sem.at[1])
    load_mom = pltpu.make_async_copy(mom_ref, mom, load_sem.at[2])
    load_in.start()

    barrier = pltpu.get_barrier_semaphore()
    partners = [dev(x_=rot(x, d)) for d in (1, 2, 3)] + [dev(z_=rot(z, d)) for d in (1, 2, 3)]
    partners += [other_core, other_lo, other_h, dev(h_=1 - h, lo_=1 - lo)]
    for to in partners:
        pl.semaphore_signal(barrier, inc=1, device_id=to, device_id_type=MESH)
    pl.semaphore_wait(barrier, len(partners))

    def cot_rows(zz, xx, hh):
        return cot_ref.at[pl.ds(pl.multiple_of((zz * 8 + xx * 2 + hh) * TOK, TOK), TOK)]

    def send_cot(i, carry):
        zz, xx = i // 4, i % 4
        remote(cot_rows(zz, xx, 1 - h), cot.at[1, 0, zz, xx], cots, cotr, other_h).start()
        remote(cot_rows(zz, xx, h), cot.at[1, 1, xx, zz], cots, cotr, other_h).start()
        return carry

    def load_cot(i, carry):
        zz, xx = i // 4, i % 4
        pltpu.make_async_copy(cot_rows(zz, xx, h), cot.at[0, 0, zz, xx], cot_sem).start()
        pltpu.make_async_copy(cot_rows(zz, xx, 1 - h), cot.at[0, 1, xx, zz], cot_sem).start()
        return carry

    onehot = (seg_ref[...] == lax.broadcasted_iota(jnp.int32, (DOCS, TOK), 0)).astype(jnp.float32)
    count = jnp.broadcast_to(jnp.sum(onehot, axis=1, keepdims=True), (DOCS, TOK))
    for phase, (own, size) in enumerate(((x, SIDE), (z, SIDE), (h, 2))):
        cnt[phase, 0] = count
        for d in range(1, size):
            to = (dev(x_=rot(x, d)), dev(z_=rot(z, d)), other_h)[phase]
            remote(cnt.at[phase, 0], cnt.at[phase, d], cnt_send.at[phase, d], cnt_recv.at[phase, d], to).start()
        if phase == 0:
            lax.fori_loop(0, EARLY, send_cot, 0)
        for d in range(1, size):
            to = (dev(x_=rot(x, d)), dev(z_=rot(z, d)), other_h)[phase]
            remote(cnt.at[phase, 0], cnt.at[phase, d], cnt_send.at[phase, d], cnt_recv.at[phase, d], to).wait()
            count = count + cnt[phase, d]
    tok_row = jnp.sum(onehot * (1.0 / count), axis=0, keepdims=True)
    tok_weight = jnp.transpose(jnp.broadcast_to(tok_row, (TOK, TOK)))

    load_in.wait()

    def a1(s, d):
        return remote(xa.at[s, z, x], xa.at[s, z, x], a1s.at[s, d], a1r.at[s, d], dev(x_=rot(x, d + 1)))

    def a2(s, d):
        return remote(xa.at[s, z], xa.at[s, z], a2s.at[s, d], a2r.at[s, d], dev(z_=rot(z, d + 1)))

    def b1(s, d):
        return remote(xb.at[s, x, z], xb.at[s, x, z], b1s.at[s, d], b1r.at[s, d], dev(z_=rot(z, d + 1)))

    def b2(s, d):
        return remote(xb.at[s, x], xb.at[s, x], b2s.at[s, d], b2r.at[s, d], dev(x_=rot(x, d + 1)))

    def cross(s):
        return remote(ysend.at[s], xb.at[s, x, z], ys.at[s], yr.at[s], other_h)

    def weigh(s, carry):
        for part in (0, 1):
            for half in (0, 1):
                hh = h if half == 0 else 1 - h
                at = pl.multiple_of(hh * HALF + part * OWN + s * BLOCK, BLOCK)
                w = (xin[:, pl.ds(at, BLOCK)].astype(jnp.float32) * tok_weight).astype(jnp.bfloat16)
                if half == 0:
                    xa[s, z, x, :, part * BLOCK : (part + 1) * BLOCK] = w
                else:
                    ysend[s, :, part * BLOCK : (part + 1) * BLOCK] = w
        cross(s).start()
        for d in range(3):
            a1(s, d).start()
        return carry

    lax.fori_loop(0, STEPS, weigh, 0)
    lax.fori_loop(0, 16, load_cot, 0)
    load_base.start()
    load_mom.start()

    def relay(s, carry):
        @pl.when(s < STEPS)
        def _():
            for d in range(3):
                a1(s, d).wait_recv()
            for d in range(3):
                a2(s, d).start()
            cross(s).wait_recv()
            for d in range(3):
                b1(s, d).start()

        @pl.when(s >= 1)
        def _():
            for d in range(3):
                b1(s - 1, d).wait_recv()
            for d in range(3):
                b2(s - 1, d).start()

        return carry

    lax.fori_loop(EARLY, 16, send_cot, 0)
    lax.fori_loop(0, STEPS + 1, relay, 0)
    pltpu.make_async_copy(cot.at[0], cot.at[0], cot_sem).wait()

    def swap(j):
        return remote(xs.at[j], xr.at[j], xss.at[j], xsr.at[j], other_core)

    def to_owner(j, s, w):
        c = jnp.where(w == 0, h, 1 - h)
        return remote(ps.at[j], rr.at[s, lo], pss.at[j], psr.at[s, lo], dev(h_=c, lo_=h))

    def from_owner(s, src):
        return remote(ps.at[0], rr.at[s, src], pss.at[0], psr.at[s, src], other_lo)

    def rows(rp, s):
        return pl.ds(pl.multiple_of(rp * OWN + s * BLOCK, BLOCK), BLOCK)

    def w_core(s):
        return remote(wt.at[s], w_out.at[rows(rep, s)], wcs.at[s], wcr.at[s], other_core)

    def w_lo(s):
        return remote(wt.at[s], w_out.at[rows(rep, s)], wls.at[s], wlr.at[s], other_lo)

    def w_fwd(s):
        there = rows((1 - lo) * 2 + core, s)
        return remote(w_out.at[there], w_out.at[there], wfs.at[s], wfr.at[s], other_core)

    def quantized(at):
        blk = inner_rate * acc[pl.ds(pl.multiple_of(at * BLOCK, BLOCK), BLOCK), :]
        scale = (jnp.max(jnp.abs(blk), axis=0, keepdims=True) + epsilon).astype(jnp.bfloat16)
        scale = scale.astype(jnp.float32)
        coded = (blk * (1.0 / scale)).astype(jnp.bfloat16)
        return coded.astype(jnp.float32) * scale

    def step(j, carry):
        @pl.when(j < 2 * STEPS)
        def _():
            w, s = j // STEPS, j % STEPS

            @pl.when(j < STEPS)
            def _():
                for d in range(3):
                    a2(s, d).wait_recv()
                    b2(s, d).wait_recv()

            @pl.when(j == STEPS)
            def _():
                pltpu.make_async_copy(cot.at[1], cot.at[1], cotr).wait()

            acc[...] = jnp.zeros_like(acc)

            def part_a(k, c):
                acc[...] += lax.dot_general(
                    xa[s, k].reshape(SIDE * TOK, 2 * BLOCK), cot[w, 0, k].reshape(SIDE * TOK, COLS),
                    (((0,), (0,)), ((), ())), preferred_element_type=jnp.float32,
                )
                acc[...] += lax.dot_general(
                    xb[s, k].reshape(SIDE * TOK, 2 * BLOCK), cot[w, 1, k].reshape(SIDE * TOK, COLS),
                    (((0,), (0,)), ((), ())), preferred_element_type=jnp.float32,
                )
                return c

            lax.fori_loop(0, SIDE, part_a, 0)
            xs[j] = quantized(1 - core)
            swap(j).start()

        @pl.when((j >= 1) & (j <= 2 * STEPS))
        def _():
            q = j - 1
            w, s = q // STEPS, q % STEPS
            swap(q).wait_recv()
            ps[q] = (keep[...] + xr[q]).astype(jnp.bfloat16)
            local = (w == 0) & (lo == h)

            @pl.when(local)
            def _():
                rr[s, lo] = ps[q]

            @pl.when(jnp.logical_not(local))
            def _():
                to_owner(q, s, w).start()

        @pl.when(j < 2 * STEPS)
        def _():
            keep[...] = quantized(core)

        @pl.when(j == STEPS)
        def _():
            load_base.wait()
            load_mom.wait()

        @pl.when((j >= STEPS + 3) & (j < 2 * STEPS + 3))
        def _():
            s = j - (STEPS + 3)
            from_owner(s, 1 - lo).wait_recv()

            @pl.when(lo != h)
            def _():
                from_owner(s, lo).wait_recv()

            average = (rr[s, 0].astype(jnp.float32) + rr[s, 1].astype(jnp.float32)) * 0.25
            at = pl.ds(pl.multiple_of(s * BLOCK, BLOCK), BLOCK)
            nm = nesterov_coef * mom[at, :] + average
            nb = base[at, :] - outer_rate * (average + nesterov_coef * nm)
            mom[at, :] = nm
            base[at, :] = nb
            wt[s] = nb.astype(jnp.bfloat16)
            w_lo(s).start()
            w_core(s).start()
            pltpu.make_async_copy(wt.at[s], w_out.at[rows(rep, s)], out_sem.at[0, s]).start()
            pltpu.make_async_copy(mom.at[at], nm_out.at[at], out_sem.at[1, s]).start()
            pltpu.make_async_copy(base.at[at], nb_out.at[at], out_sem.at[2, s]).start()

        @pl.when(j >= STEPS + 5)
        def _():
            s = j - (STEPS + 5)
            w_lo(s).wait_recv()
            w_fwd(s).start()

        return carry

    lax.fori_loop(0, 2 * STEPS + 5, step, 0)

    def finish(s, carry):
        for d in range(3):
            a1(s, d).wait_send()
            a2(s, d).wait_send()
            b1(s, d).wait_send()
            b2(s, d).wait_send()
        cross(s).wait_send()
        swap(s).wait_send()
        swap(s + STEPS).wait_send()

        @pl.when(lo != h)
        def _():
            to_owner(s, s, 0).wait_send()

        to_owner(s + STEPS, s, 1).wait_send()
        w_core(s).wait_send()
        w_lo(s).wait_send()
        w_fwd(s).wait_send()
        w_core(s).wait_recv()
        w_fwd(s).wait_recv()
        at = pl.ds(pl.multiple_of(s * BLOCK, BLOCK), BLOCK)
        pltpu.make_async_copy(wt.at[s], w_out.at[rows(rep, s)], out_sem.at[0, s]).wait()
        pltpu.make_async_copy(mom.at[at], nm_out.at[at], out_sem.at[1, s]).wait()
        pltpu.make_async_copy(base.at[at], nb_out.at[at], out_sem.at[2, s]).wait()
        return carry

    lax.fori_loop(0, STEPS, finish, 0)
    pltpu.make_async_copy(cot.at[1], cot.at[1], cots).wait()


def body(inputs, segments, cotangent, base, momentum):
    bf, f32, dma = jnp.bfloat16, jnp.float32, pltpu.SemaphoreType.DMA
    hbm = pl.BlockSpec(memory_space=pl.ANY)
    return pl.pallas_call(
        kernel,
        out_shape=(
            jax.ShapeDtypeStruct((OWN, COLS), f32),
            jax.ShapeDtypeStruct((OWN, COLS), f32),
            jax.ShapeDtypeStruct((D, COLS), bf),
        ),
        in_specs=[pl.BlockSpec(memory_space=pltpu.VMEM), hbm, hbm, hbm, hbm],
        out_specs=(hbm, hbm, hbm),
        scratch_shapes=[
            pltpu.VMEM((TOK, D), bf),
            pltpu.VMEM((STEPS, SIDE, SIDE, TOK, 2 * BLOCK), bf),
            pltpu.VMEM((STEPS, SIDE, SIDE, TOK, 2 * BLOCK), bf),
            pltpu.VMEM((STEPS, TOK, 2 * BLOCK), bf),
            pltpu.VMEM((2, 2, SIDE, SIDE, TOK, COLS), bf),
            pltpu.VMEM((OWN, COLS), f32),
            pltpu.VMEM((OWN, COLS), f32),
            pltpu.VMEM((2 * BLOCK, COLS), f32),
            pltpu.VMEM((BLOCK, COLS), f32),
            pltpu.VMEM((2 * STEPS, BLOCK, COLS), f32),
            pltpu.VMEM((2 * STEPS, BLOCK, COLS), f32),
            pltpu.VMEM((2 * STEPS, BLOCK, COLS), bf),
            pltpu.VMEM((STEPS, 2, BLOCK, COLS), bf),
            pltpu.VMEM((STEPS, BLOCK, COLS), bf),
            pltpu.VMEM((3, SIDE, DOCS, TOK), f32),
            dma((3,)), dma, dma((3, SIDE)), dma((3, SIDE)),
            dma((STEPS, 3)), dma((STEPS, 3)), dma((STEPS, 3)), dma((STEPS, 3)),
            dma((STEPS, 3)), dma((STEPS, 3)), dma((STEPS, 3)), dma((STEPS, 3)),
            dma((STEPS,)), dma((STEPS,)), dma, dma,
            dma((2 * STEPS,)), dma((2 * STEPS,)), dma((2 * STEPS,)), dma((STEPS, 2)),
            dma((STEPS,)), dma((STEPS,)), dma((STEPS,)), dma((STEPS,)),
            dma((STEPS,)), dma((STEPS,)), dma((3, STEPS)),
        ],
        compiler_params=pltpu.CompilerParams(
            collective_id=0, has_side_effects=True, vmem_limit_bytes=60 * 2**20
        ),
        cost_estimate=pl.CostEstimate(flops=2 * D * D * COLS, bytes_accessed=2**24, transcendentals=0),
    )(segments, inputs[0], cotangent[0], base, momentum)


def solution(mesh):
    return jax.shard_map(
        body,
        mesh=mesh,
        in_specs=(
            P("replica", "fsdp", None),
            P("replica", "fsdp"),
            P("replica", None, "fsdp"),
            P("replica", "fsdp"),
            P("replica", "fsdp"),
        ),
        out_specs=(P("replica", "fsdp"), P("replica", "fsdp"), P(None, "fsdp")),
        check_vma=False,
    )
```

```python
import jax
import jax.numpy as jnp
from jax import lax
from jax.experimental import pallas as pl
from jax.experimental.pallas import tpu as pltpu
from jax.sharding import PartitionSpec as P

D = 4096
BLOCK = 128
DOCS = 16
STEPS = 8
SIDE = 4
TOK = 128
TOK_G = 4096
COLS = 448
HALF = D // 2
OWN = D // 4
DEPTH = 1024
SWAP = 1024
PART = COLS // 2
TILES = 2 * STEPS
UNITS = 4 * STEPS
PASS = 2
SHIP = UNITS - TILES + 5
AHEAD = 4

inner_rate = 2.0
outer_rate = 0.7
nesterov_coef = 0.9
epsilon = 1e-06
MESH = pl.DeviceIdType.MESH


def kernel(
    seg_ref, inp_ref, cot_ref, base_ref, mom_ref,
    nb_out, nm_out, w_out,
    xg, ysend, cot, base, mom, acc, keep, xs, xr, ps, rr, wt, segs, weight,
    load_sem, in_sem, seg_send, seg_recv,
    a1s, a1r, a2s, a2r, a3s, a3r, b1s, b1r, b2s, b2r, b3s, b3r, ys, yr, cots, cotr,
    xss, xsr, pss, psr, wcs, wcr, wls, wlr, wfs, wfr, out_sem,
):
    rep, f = lax.axis_index("replica"), lax.axis_index("fsdp")
    lo, core = rep // 2, rep % 2
    z, x, h = f // 8, (f // 2) % 4, f % 2

    def dev(x_=x, z_=z, h_=h, lo_=lo, core_=core):
        return (lo_ * 2 + core_, z_ * 8 + x_ * 2 + h_)

    def rot(v, d):
        return lax.rem(v + d, SIDE)

    other_core = dev(core_=1 - core)
    other_lo = dev(lo_=1 - lo)
    other_h = dev(h_=1 - h)
    along_x = [dev(x_=rot(x, d)) for d in (1, 2, 3)]
    along_z = [dev(z_=rot(z, d)) for d in (1, 2, 3)]

    def remote(src, dst, ss, rs, to):
        return pltpu.make_async_remote_copy(
            src_ref=src, dst_ref=dst, send_sem=ss, recv_sem=rs, device_id=to, device_id_type=MESH
        )

    def lanes(at, size=BLOCK):
        return pl.ds(pl.multiple_of(at, BLOCK), size)

    def load_rows(s, part, half):
        hh = h if half == 0 else 1 - h
        dst = xg.at[s, z, x, h] if half == 0 else ysend.at[s]
        return pltpu.make_async_copy(
            inp_ref.at[:, lanes(hh * HALF + part * OWN + s * BLOCK)],
            dst.at[:, part * BLOCK : (part + 1) * BLOCK],
            in_sem.at[s, part, half],
        )

    def load_all(s, carry):
        for part in (0, 1):
            for half in (0, 1):
                load_rows(s, part, half).start()
        return carry

    lax.fori_loop(0, STEPS, load_all, 0)
    def load_cot(u):
        return pltpu.make_async_copy(cot_ref.at[u * PART : (u + 1) * PART], cot.at[u], load_sem.at[2 + u])

    load_base = pltpu.make_async_copy(base_ref, base, load_sem.at[0])
    load_mom = pltpu.make_async_copy(mom_ref, mom, load_sem.at[1])
    segs[z, x, h] = jnp.broadcast_to(seg_ref[...], (8, TOK))

    barrier = pltpu.get_barrier_semaphore()
    partners = along_x + along_z + [other_core, other_lo, other_h, dev(h_=1 - h, lo_=1 - lo)]
    for to in partners:
        pl.semaphore_signal(barrier, inc=1, device_id=to, device_id_type=MESH)
    pl.semaphore_wait(barrier, len(partners))

    seg_h = remote(segs.at[z, x, h], segs.at[z, x, h], seg_send.at[2, 0], seg_recv.at[2, 0], other_h)

    def seg_x(d):
        return remote(segs.at[z, x], segs.at[z, x], seg_send.at[0, d], seg_recv.at[0, d], along_x[d])

    def seg_z(d):
        return remote(segs.at[z], segs.at[z], seg_send.at[1, d], seg_recv.at[1, d], along_z[d])

    def cross(s):
        return remote(ysend.at[s], xg.at[s, z, x, h], ys.at[s], yr.at[s], other_h)

    def a1(s, d):
        ref = xg.at[s, z, x, h]
        return remote(ref, ref, a1s.at[s, d], a1r.at[s, d], along_x[d])

    def a2(s, d):
        ref = xg.at[s, z, :, h]
        return remote(ref, ref, a2s.at[s, d], a2r.at[s, d], along_z[2 * d])

    def a3(s, d):
        ref = xg.at[s, rot(z, 3 - 2 * d), 2 * d : 2 * d + 2, h]
        return remote(ref, ref, a3s.at[s, d], a3r.at[s, d], along_z[2 * d])

    def b1(s, d):
        ref = xg.at[s, z, x, 1 - h]
        return remote(ref, ref, b1s.at[s, d], b1r.at[s, d], along_z[d])

    def b2(s, d):
        ref = xg.at[s, :, x, 1 - h]
        return remote(ref, ref, b2s.at[s, d], b2r.at[s, d], along_x[2 * d])

    def b3(s, d):
        ref = xg.at[s, 2 * d : 2 * d + 2, rot(x, 3 - 2 * d), 1 - h]
        return remote(ref, ref, b3s.at[s, d], b3r.at[s, d], along_x[2 * d])

    seg_h.start()

    def first(s, carry):
        for part in (0, 1):
            load_rows(s, part, 1).wait()
        cross(s).start()
        return carry

    def start_own(s):
        for part in (0, 1):
            load_rows(s, part, 0).wait()
        for d in range(3):
            a1(s, d).start()

    def tick(i):
        def at(s, body):
            @pl.when((s >= 0) & (s < STEPS))
            def _():
                body(s)

        def own2(s):
            for d in range(3):
                a1(s, d).wait_recv()
            for d in range(2):
                a2(s, d).start()

        def partner1(s):
            cross(s).wait_recv()
            for d in range(3):
                b1(s, d).start()

        def own3(s):
            for d in range(2):
                a2(s, d).wait_recv()
            for d in range(2):
                a3(s, d).start()

        def partner2(s):
            for d in range(3):
                b1(s, d).wait_recv()
            for d in range(2):
                b2(s, d).start()

        def partner3(s):
            for d in range(2):
                b2(s, d).wait_recv()
            for d in range(2):
                b3(s, d).start()

        at(i + 1, start_own)
        at(i - 1, own2)
        at(i - 1, partner1)
        at(i - 2, own3)
        at(i - 2, partner2)
        at(i - 3, partner3)

    start_own(0)
    lax.fori_loop(0, STEPS, first, 0)

    def send_cot(u):
        def go(i, carry):
            at = lanes(i * SWAP, SWAP)
            remote(cot_ref.at[u * PART : (u + 1) * PART, at], cot.at[2 + u, :, at], cots.at[u], cotr.at[u], other_h).start()
            return carry

        lax.fori_loop(0, TOK_G // SWAP, go, 0)

    send_cot(0)
    send_cot(1)
    seg_h.wait_recv()
    for d in range(3):
        seg_x(d).start()
    tick(0)
    load_cot(0).start()
    load_cot(1).start()
    load_base.start()
    load_mom.start()
    for d in range(3):
        seg_x(d).wait_recv()
    for d in range(3):
        seg_z(d).start()
    tick(1)
    tick(2)
    for d in range(3):
        seg_z(d).wait_recv()
    tick(3)

    ids = segs[...].reshape(TOK_G // TOK, 8, TOK)
    per_token = jnp.zeros((TOK_G // TOK, 8, TOK), jnp.float32)
    for doc in range(DOCS):
        mine = (ids == doc).astype(jnp.float32)
        count = jnp.sum(jnp.sum(mine, axis=0), axis=1, keepdims=True)
        per_token = per_token + mine * (1.0 / count)[None]
    weight[...] = per_token

    def scale_cot(g):
        def tile(i, carry):
            at = lanes(i * TOK)
            raw = cot[g, :, at].astype(jnp.float32).reshape(PART // 8, 8, TOK)
            cot[g, :, at] = (raw * weight[i][None]).reshape(PART, TOK).astype(jnp.bfloat16)
            return carry

        lax.fori_loop(0, TOK_G // TOK, tile, 0)

    for u in (0, 1):
        load_cot(u).wait()
        scale_cot(u)

    def swap(j):
        return remote(xs.at[j], xr.at[j], xss.at[j], xsr.at[j], other_core)

    def to_owner(j, g, s):
        c = jnp.where(g < 2, h, 1 - h)
        k = (g % 2) * STEPS + s
        return remote(ps.at[j], rr.at[k, lo], pss.at[j], psr.at[k, lo], dev(h_=c, lo_=h))

    def from_owner(k, src):
        return remote(ps.at[0], rr.at[k, src], pss.at[0], psr.at[k, src], other_lo)

    def place(k, ref, rp=None):
        u, s = k // STEPS, k % STEPS
        first = s * BLOCK if rp is None else rp * OWN + s * BLOCK
        return ref.at[pl.ds(pl.multiple_of(u * PART, 32), PART), lanes(first)]

    def w_core(k):
        return remote(wt.at[k], place(k, w_out, rep), wcs.at[k], wcr.at[k], other_core)

    def w_lo(k):
        return remote(wt.at[k], place(k, w_out, rep), wls.at[k], wlr.at[k], other_lo)

    def w_fwd(k):
        there = place(k, w_out, (1 - lo) * 2 + core)
        return remote(there, there, wfs.at[k], wfr.at[k], other_core)

    def w_own(k):
        return pltpu.make_async_copy(wt.at[k], place(k, w_out, rep), out_sem.at[0, k])

    def nm_own(k):
        return pltpu.make_async_copy(place(k, mom), place(k, nm_out), out_sem.at[1, k])

    def nb_own(k):
        return pltpu.make_async_copy(place(k, base), place(k, nb_out), out_sem.at[2, k])

    def quantized(at):
        blk = inner_rate * acc[:, lanes(at * BLOCK)]
        scale = (jnp.max(jnp.abs(blk), axis=1, keepdims=True) + epsilon).astype(jnp.bfloat16)
        scale = scale.astype(jnp.float32)
        coded = (blk * (1.0 / scale)).astype(jnp.bfloat16)
        return coded.astype(jnp.float32) * scale

    def unit(j):
        t = j - 15
        g = jnp.where(j < 10, j % 2, jnp.where(j < 15, 2, jnp.where(j < 24, t % 3, 3)))
        s = jnp.where(j < 10, j // 2, jnp.where(j < 15, j - 10, jnp.where(j < 24, 5 + t // 3, j - 24)))
        return g, s

    def step(j, carry):
        @pl.when(j < UNITS)
        def _():
            g, s = unit(j)

            @pl.when(g == 0)
            def _():
                tick(s + AHEAD)
                for d in range(2):
                    a3(s, d).wait_recv()
                    b3(s, d).wait_recv()

            for u, at in ((0, 10), (1, 24)):

                @pl.when(j == at)
                def _():
                    got = cot.at[2 + u]
                    pltpu.make_async_copy(got, got, cotr.at[u]).wait()
                    scale_cot(2 + u)

            def part(k, c):
                prod = jnp.dot(
                    cot[g, :, lanes(k * DEPTH, DEPTH)],
                    xg[s, k].reshape(DEPTH, 2 * BLOCK),
                    preferred_element_type=jnp.float32,
                )

                @pl.when(k == 0)
                def _():
                    acc[...] = prod

                @pl.when(k > 0)
                def _():
                    acc[...] += prod

                return c

            lax.fori_loop(0, TOK_G // DEPTH, part, 0)
            xs[j] = quantized(1 - core)
            swap(j).start()
            keep[j % 4] = quantized(core)

        @pl.when((j >= PASS) & (j < UNITS + PASS))
        def _():
            q = j - PASS
            g, s = unit(q)
            swap(q).wait_recv()
            ps[q] = (keep[q % 4] + xr[q]).astype(jnp.bfloat16)
            local = (g < 2) & (lo == h)

            @pl.when(local)
            def _():
                rr[g * STEPS + s, lo] = ps[q]

            @pl.when(jnp.logical_not(local))
            def _():
                to_owner(q, g, s).start()

        @pl.when(j == SHIP)
        def _():
            load_base.wait()
            load_mom.wait()

        @pl.when((j >= SHIP) & (j < SHIP + TILES))
        def _():
            k = j - SHIP
            from_owner(k, 1 - lo).wait_recv()

            @pl.when(lo != h)
            def _():
                from_owner(k, lo).wait_recv()

            average = (rr[k, 0].astype(jnp.float32) + rr[k, 1].astype(jnp.float32)) * 0.25
            u, s = k // STEPS, k % STEPS
            cols, at = pl.ds(pl.multiple_of(u * PART, 32), PART), lanes(s * BLOCK)
            nm = nesterov_coef * mom[cols, at] + average
            nb = base[cols, at] - outer_rate * (average + nesterov_coef * nm)
            wt[k] = nb.astype(jnp.bfloat16)
            w_lo(k).start()
            w_core(k).start()
            mom[cols, at] = nm
            base[cols, at] = nb
            w_own(k).start()
            nm_own(k).start()
            nb_own(k).start()

        @pl.when(j >= SHIP + 3)
        def _():
            k = j - (SHIP + 3)
            w_lo(k).wait_recv()
            w_fwd(k).start()

        return carry

    lax.fori_loop(0, SHIP + 3 + TILES, step, 0)

    for d in range(3):
        seg_x(d).wait_send()
        seg_z(d).wait_send()
    seg_h.wait_send()

    def finish(s, carry):
        for d in range(3):
            a1(s, d).wait_send()
            b1(s, d).wait_send()
        for d in range(2):
            a2(s, d).wait_send()
            b2(s, d).wait_send()
            a3(s, d).wait_send()
            b3(s, d).wait_send()
        cross(s).wait_send()
        return carry

    lax.fori_loop(0, STEPS, finish, 0)

    def finish_units(q, carry):
        g, s = unit(q)
        swap(q).wait_send()

        @pl.when(jnp.logical_not((g < 2) & (lo == h)))
        def _():
            to_owner(q, g, s).wait_send()

        return carry

    lax.fori_loop(0, UNITS, finish_units, 0)
    for u in (0, 1):
        pltpu.make_async_copy(cot.at[2 + u], cot.at[2 + u], cots.at[u]).wait()

    def finish_tiles(k, carry):
        w_core(k).wait_send()
        w_lo(k).wait_send()
        w_own(k).wait()
        nm_own(k).wait()
        nb_own(k).wait()
        w_core(k).wait_recv()
        w_fwd(k).wait_send()
        w_fwd(k).wait_recv()
        return carry

    lax.fori_loop(0, TILES, finish_tiles, 0)


def body(inputs, segments, cotangent, base, momentum):
    bf, f32, dma = jnp.bfloat16, jnp.float32, pltpu.SemaphoreType.DMA
    hbm = pl.BlockSpec(memory_space=pl.ANY)
    nb, nm, w = pl.pallas_call(
        kernel,
        out_shape=(
            jax.ShapeDtypeStruct((COLS, OWN), f32),
            jax.ShapeDtypeStruct((COLS, OWN), f32),
            jax.ShapeDtypeStruct((COLS, D), bf),
        ),
        in_specs=[pl.BlockSpec(memory_space=pltpu.VMEM), hbm, hbm, hbm, hbm],
        out_specs=(hbm, hbm, hbm),
        scratch_shapes=[
            pltpu.VMEM((STEPS, SIDE, SIDE, 2, TOK, 2 * BLOCK), bf),
            pltpu.VMEM((STEPS, TOK, 2 * BLOCK), bf),
            pltpu.VMEM((4, PART, TOK_G), bf),
            pltpu.VMEM((COLS, OWN), f32),
            pltpu.VMEM((COLS, OWN), f32),
            pltpu.VMEM((PART, 2 * BLOCK), f32),
            pltpu.VMEM((4, PART, BLOCK), f32),
            pltpu.VMEM((UNITS, PART, BLOCK), f32),
            pltpu.VMEM((UNITS, PART, BLOCK), f32),
            pltpu.VMEM((UNITS, PART, BLOCK), bf),
            pltpu.VMEM((TILES, 2, PART, BLOCK), bf),
            pltpu.VMEM((TILES, PART, BLOCK), bf),
            pltpu.VMEM((SIDE, SIDE, 2, 8, TOK), jnp.int32),
            pltpu.VMEM((TOK_G // TOK, 8, TOK), f32),
            dma((4,)), dma((STEPS, 2, 2)), dma((3, 3)), dma((3, 3)),
            dma((STEPS, 3)), dma((STEPS, 3)), dma((STEPS, 2)), dma((STEPS, 2)), dma((STEPS, 2)), dma((STEPS, 2)),
            dma((STEPS, 3)), dma((STEPS, 3)), dma((STEPS, 2)), dma((STEPS, 2)), dma((STEPS, 2)), dma((STEPS, 2)),
            dma((STEPS,)), dma((STEPS,)), dma((2,)), dma((2,)),
            dma((UNITS,)), dma((UNITS,)), dma((UNITS,)), dma((TILES, 2)),
            dma((TILES,)), dma((TILES,)), dma((TILES,)), dma((TILES,)),
            dma((TILES,)), dma((TILES,)), dma((3, TILES)),
        ],
        compiler_params=pltpu.CompilerParams(
            collective_id=0, has_side_effects=True, vmem_limit_bytes=60 * 2**20
        ),
        cost_estimate=pl.CostEstimate(flops=2 * D * D * COLS, bytes_accessed=2**24, transcendentals=0),
    )(segments, inputs[0], cotangent[0].T, base.T, momentum.T)
    return nb.T, nm.T, w.T


def solution(mesh):
    return jax.shard_map(
        body,
        mesh=mesh,
        in_specs=(
            P("replica", "fsdp", None),
            P("replica", "fsdp"),
            P("replica", None, "fsdp"),
            P("replica", "fsdp"),
            P("replica", "fsdp"),
        ),
        out_specs=(P("replica", "fsdp"), P("replica", "fsdp"), P(None, "fsdp")),
        check_vma=False,
    )
```

```python
import jax
import jax.numpy as jnp
from jax import lax
from jax.experimental import pallas as pl
from jax.experimental.pallas import tpu as pltpu
from jax.sharding import PartitionSpec as P

D = 4096
BLOCK = 128
DOCS = 16
STEPS = 8
SIDE = 4
TOK = 128
TOK_G = 4096
COLS = 448
HALF = D // 2
OWN = D // 4
DEPTH = 1024
SWAP = 1024
PART = COLS // 2
TILES = 2 * STEPS
UNITS = 4 * STEPS
PASS = 2
SHIP = UNITS - TILES + 5
AHEAD = 3

inner_rate = 2.0
outer_rate = 0.7
nesterov_coef = 0.9
epsilon = 1e-06
MESH = pl.DeviceIdType.MESH


def kernel(
    seg_ref, inp_ref, cot_ref, base_ref, mom_ref,
    nb_out, nm_out, w_out,
    xg, ysend, raw, cot, base, mom, acc, keep, xs, xr, ps, rr, wt, seg_own, segs, weight,
    load_sem, in_sem, seg_send, seg_recv,
    a1s, a1r, a2s, a2r, a3s, a3r, b1s, b1r, b2s, b2r, b3s, b3r, ys, yr, cots, cotr, rawr, fwds,
    xss, xsr, pss, psr, wcs, wcr, wls, wlr, wfs, wfr, out_sem,
):
    rep, f = lax.axis_index("replica"), lax.axis_index("fsdp")
    lo, core = rep // 2, rep % 2
    z, x, h = f // 8, (f // 2) % 4, f % 2

    def dev(x_=x, z_=z, h_=h, lo_=lo, core_=core):
        return (lo_ * 2 + core_, z_ * 8 + x_ * 2 + h_)

    def rot(v, d):
        return lax.rem(v + d, SIDE)

    other_core = dev(core_=1 - core)
    other_lo = dev(lo_=1 - lo)
    other_h = dev(h_=1 - h)
    across = dev(h_=1 - h, lo_=1 - lo)
    at_home = (h + core) % 2 == 0
    helper = dev(h_=jnp.where(at_home, 1 - h, h), lo_=1 - lo)
    along_x = [dev(x_=rot(x, d)) for d in (1, 2, 3)]
    along_z = [dev(z_=rot(z, d)) for d in (1, 2, 3)]

    def remote(src, dst, ss, rs, to):
        return pltpu.make_async_remote_copy(
            src_ref=src, dst_ref=dst, send_sem=ss, recv_sem=rs, device_id=to, device_id_type=MESH
        )

    def lanes(at, size=BLOCK):
        return pl.ds(pl.multiple_of(at, BLOCK), size)

    def load_rows(s, part, half, stay=False):
        hh = lo if half == 0 else 1 - lo
        dst = xg.at[s, z, x, h] if stay else ysend.at[half, s]
        return pltpu.make_async_copy(
            inp_ref.at[:, lanes(hh * HALF + part * OWN + s * BLOCK)],
            dst.at[:, part * BLOCK : (part + 1) * BLOCK],
            in_sem.at[s, part, half],
        )

    def load_all(s, carry):
        for part in (0, 1):
            load_rows(s, part, 0).start()

            @pl.when(at_home)
            def _():
                load_rows(s, part, 1, True).start()

            @pl.when(jnp.logical_not(at_home))
            def _():
                load_rows(s, part, 1).start()

        return carry

    lax.fori_loop(0, STEPS, load_all, 0)
    def load_cot(u):
        return pltpu.make_async_copy(cot_ref.at[u * PART : (u + 1) * PART], raw.at[u], load_sem.at[2 + u])

    load_base = pltpu.make_async_copy(base_ref, base, load_sem.at[0])
    load_mom = pltpu.make_async_copy(mom_ref, mom, load_sem.at[1])
    seg_own[...] = jnp.broadcast_to(seg_ref[...], (8, TOK))

    @pl.when(at_home)
    def _():
        segs[z, x, h] = jnp.broadcast_to(seg_ref[...], (8, TOK))

    barrier = pltpu.get_barrier_semaphore()
    partners = along_x + along_z + [other_core, other_lo, other_h, across]
    for to in partners:
        pl.semaphore_signal(barrier, inc=1, device_id=to, device_id_type=MESH)
    pl.semaphore_wait(barrier, len(partners))

    far = jnp.where(at_home, 0, 1)

    def seg_help(kind):
        return remote(seg_own, segs.at[z, x, h], seg_send.at[2, 0], seg_recv.at[2, kind], helper)

    seg_native = remote(seg_own, segs.at[z, x, h], seg_send.at[2, 1], seg_recv.at[2, 0], other_h)

    def seg_x(d):
        return remote(segs.at[z, x], segs.at[z, x], seg_send.at[0, d], seg_recv.at[0, d], along_x[d])

    def seg_z(d):
        return remote(segs.at[z], segs.at[z], seg_send.at[1, d], seg_recv.at[1, d], along_z[d])

    def cross_help(s, kind):
        return remote(ysend.at[0, s], xg.at[s, z, x, h], ys.at[0], yr.at[s, kind], helper)

    def cross_native(s):
        return remote(ysend.at[1, s], xg.at[s, z, x, h], ys.at[1], yr.at[s, 0], other_h)

    def a1(s, d):
        ref = xg.at[s, z, x, h]
        return remote(ref, ref, a1s, a1r.at[s, d], along_x[d])

    def a2(s, d):
        ref = xg.at[s, z, :, h]
        return remote(ref, ref, a2s, a2r.at[s, d], along_z[2 * d])

    def a3(s, d):
        ref = xg.at[s, rot(z, 3 - 2 * d), 2 * d : 2 * d + 2, h]
        return remote(ref, ref, a3s, a3r.at[s, d], along_z[2 * d])

    def b1(s, d):
        ref = xg.at[s, z, x, 1 - h]
        return remote(ref, ref, b1s, b1r.at[s, d], along_z[d])

    def b2(s, d):
        ref = xg.at[s, :, x, 1 - h]
        return remote(ref, ref, b2s, b2r.at[s, d], along_x[2 * d])

    def b3(s, d):
        ref = xg.at[s, 2 * d : 2 * d + 2, rot(x, 3 - 2 * d), 1 - h]
        return remote(ref, ref, b3s, b3r.at[s, d], along_x[2 * d])

    def away(body):
        pl.when(jnp.logical_not(at_home))(body)

    seg_help(far).start()
    away(lambda: seg_native.start())

    def first(s, carry):
        for part in (0, 1):
            load_rows(s, part, 0).wait()
        cross_help(s, far).start()

        @pl.when(jnp.logical_not(at_home))
        def _():
            for part in (0, 1):
                load_rows(s, part, 1).wait()
            cross_native(s).start()

        return carry

    def start_own(s):
        @pl.when(at_home)
        def _():
            for part in (0, 1):
                load_rows(s, part, 1, True).wait()

        @pl.when(jnp.logical_not(at_home))
        def _():
            cross_help(s, 1).wait_recv()

        for d in range(3):
            a1(s, d).start()

    def partner1(s):
        cross_help(s, 0).wait_recv()
        for d in range(3):
            b1(s, d).start()

    def tick(i):
        def at(s, body):
            @pl.when((s >= 0) & (s < STEPS))
            def _():
                body(s)

        def own2(s):
            for d in range(3):
                a1(s, d).wait_recv()
            for d in range(2):
                a2(s, d).start()

        def own3(s):
            for d in range(2):
                a2(s, d).wait_recv()
            for d in range(2):
                a3(s, d).start()

        def partner2(s):
            for d in range(3):
                b1(s, d).wait_recv()
            for d in range(2):
                b2(s, d).start()

        def partner3(s):
            for d in range(2):
                b2(s, d).wait_recv()
            for d in range(2):
                b3(s, d).start()

        at(i - 2, own3)
        at(i - 2, partner3)
        at(i - 1, own2)
        at(i - 1, partner2)
        at(i + 1, partner1)
        at(i + 3, start_own)

    def send_cot(u):
        @pl.when(at_home)
        def _():
            def go(i, carry):
                at = lanes(i * SWAP, SWAP)
                remote(cot_ref.at[u * PART : (u + 1) * PART, at], cot.at[2 + u, :, at], cots.at[u], cotr.at[u], across).start()
                return carry

            lax.fori_loop(0, TOK_G // SWAP, go, 0)

        @pl.when(jnp.logical_not(at_home))
        def _():
            def go(i, carry):
                at = lanes(i * SWAP, SWAP)
                remote(cot_ref.at[u * PART : (u + 1) * PART, at], raw.at[u, :, at], cots.at[u], rawr.at[u, i], other_lo).start()
                return carry

            lax.fori_loop(0, TOK_G // SWAP, go, 0)

    def pass_cot(u, first, last):
        @pl.when(jnp.logical_not(at_home))
        def _():
            def go(i, carry):
                at = lanes(i * SWAP, SWAP)
                remote(raw.at[u, :, at], raw.at[u, :, at], cots.at[u], rawr.at[u, i], other_lo).wait_recv()
                remote(raw.at[u, :, at], cot.at[2 + u, :, at], fwds.at[u], cotr.at[u], across).start()
                return carry

            lax.fori_loop(first, last, go, 0)

    lax.fori_loop(0, STEPS, first, 0)
    send_cot(0)
    send_cot(1)
    start_own(0)
    partner1(0)
    start_own(1)
    start_own(2)
    seg_help(0).wait_recv()
    away(lambda: seg_help(1).wait_recv())
    for d in range(3):
        seg_x(d).start()
    tick(0)

    @pl.when(at_home)
    def _():
        load_cot(0).start()
        load_cot(1).start()

    load_base.start()
    load_mom.start()
    for d in range(3):
        seg_x(d).wait_recv()
    for d in range(3):
        seg_z(d).start()
    tick(1)
    tick(2)
    for d in range(3):
        seg_z(d).wait_recv()
    pass_cot(0, 0, 2)
    tick(3)
    pass_cot(0, 2, TOK_G // SWAP)

    ids = segs[...].reshape(TOK_G // TOK, 8, TOK)
    per_token = jnp.zeros((TOK_G // TOK, 8, TOK), jnp.float32)
    for doc in range(DOCS):
        mine = (ids == doc).astype(jnp.float32)
        count = jnp.sum(jnp.sum(mine, axis=0), axis=1, keepdims=True)
        per_token = per_token + mine * (1.0 / count)[None]
    weight[...] = per_token

    def scale_cot(src, g):
        def tile(i, carry):
            at = lanes(i * TOK)
            block = src[:, at].astype(jnp.float32).reshape(PART // 8, 8, TOK)
            cot[g, :, at] = (block * weight[i][None]).reshape(PART, TOK).astype(jnp.bfloat16)
            return carry

        lax.fori_loop(0, TOK_G // TOK, tile, 0)

    def scale_own(u):
        @pl.when(at_home)
        def _():
            load_cot(u).wait()

        scale_cot(raw.at[u], u)

    scale_own(0)

    def swap(j):
        return remote(xs.at[j], xr.at[j], xss, xsr.at[j], other_core)

    def to_owner(j, g, s):
        k, side = (g % 2) * STEPS + s, g // 2
        return remote(ps.at[j], rr.at[k, side], pss, psr.at[k, side], dev(h_=jnp.where(g < 2, h, 1 - h), lo_=1 - lo))

    def from_owner(k, side):
        return remote(ps.at[0], rr.at[k, side], pss, psr.at[k, side], other_lo)

    def place(k, ref, rp=None):
        u, s = k // STEPS, k % STEPS
        first = s * BLOCK if rp is None else rp * OWN + s * BLOCK
        return ref.at[pl.ds(pl.multiple_of(u * PART, 32), PART), lanes(first)]

    def w_core(k):
        return remote(wt.at[k], place(k, w_out, rep), wcs, wcr, other_core)

    def w_lo(k):
        return remote(wt.at[k], place(k, w_out, rep), wls, wlr.at[k], other_lo)

    def w_fwd(k):
        there = place(k, w_out, (1 - lo) * 2 + core)
        return remote(there, there, wfs, wfr, other_core)

    def w_own(k):
        return pltpu.make_async_copy(wt.at[k], place(k, w_out, rep), out_sem.at[0])

    def nm_own(k):
        return pltpu.make_async_copy(place(k, mom), place(k, nm_out), out_sem.at[1])

    def nb_own(k):
        return pltpu.make_async_copy(place(k, base), place(k, nb_out), out_sem.at[2])

    def quantized(at):
        blk = inner_rate * acc[:, lanes(at * BLOCK)]
        scale = (jnp.max(jnp.abs(blk), axis=1, keepdims=True) + epsilon).astype(jnp.bfloat16)
        scale = scale.astype(jnp.float32)
        coded = (blk * (1.0 / scale)).astype(jnp.bfloat16)
        return coded.astype(jnp.float32) * scale

    def pick(j, *cases):
        value = cases[-1]
        for bound, case in reversed(cases[:-1]):
            value = jnp.where(j < bound, case, value)
        return value

    def unit(j):
        g = pick(j, (6, j // 3), (10, j % 2), (15, 2), (21, j % 3), (27, 3), (30, j - 27), 3)
        s = pick(j, (6, j % 3), (10, j // 2), (15, j - 10), (21, j // 3), (27, j - 21), (30, STEPS - 1), j - 24)
        return g, s

    def tile_of(m):
        return pick(m, (7, m), (13, m + 1), (14, 7), m)

    def step(j, carry):
        @pl.when(j < UNITS)
        def _():
            g, s = unit(j)

            @pl.when(g == 0)
            def _():
                for d in range(2):
                    a3(s, d).wait_recv()
                    b3(s, d).wait_recv()

            @pl.when(j == 3)
            def _():
                pass_cot(1, 0, TOK_G // SWAP)
                scale_own(1)

            for u, at in ((0, 10), (1, 21)):

                @pl.when(j == at)
                def _():
                    got = cot.at[2 + u]
                    pltpu.make_async_copy(got, got, cotr.at[u]).wait()
                    scale_cot(got, 2 + u)

            def part(k, c):
                prod = jnp.dot(
                    cot[g, :, lanes(k * DEPTH, DEPTH)],
                    xg[s, k].reshape(DEPTH, 2 * BLOCK),
                    preferred_element_type=jnp.float32,
                )

                @pl.when(k == 0)
                def _():
                    acc[...] = prod

                @pl.when(k > 0)
                def _():
                    acc[...] += prod

                return c

            lax.fori_loop(0, TOK_G // DEPTH, part, 0)
            xs[j] = quantized(1 - core)
            swap(j).start()
            keep[j % 4] = quantized(core)

            @pl.when(((g == 0) & (s > 0) & (s < 3)) | ((g == 1) & (s >= 3)))
            def _():
                tick(s + AHEAD)

        @pl.when((j >= PASS) & (j < UNITS + PASS))
        def _():
            q = j - PASS
            g, s = unit(q)
            swap(q).wait_recv()
            ps[q] = (keep[q % 4] + xr[q]).astype(jnp.bfloat16)
            to_owner(q, g, s).start()

        @pl.when(j == SHIP)
        def _():
            load_base.wait()
            load_mom.wait()

        @pl.when((j >= SHIP) & (j < SHIP + TILES))
        def _():
            k = tile_of(j - SHIP)
            from_owner(k, 0).wait_recv()
            from_owner(k, 1).wait_recv()
            average = (rr[k, 0].astype(jnp.float32) + rr[k, 1].astype(jnp.float32)) * 0.25
            u, s = k // STEPS, k % STEPS
            cols, at = pl.ds(pl.multiple_of(u * PART, 32), PART), lanes(s * BLOCK)
            nm = nesterov_coef * mom[cols, at] + average
            nb = base[cols, at] - outer_rate * (average + nesterov_coef * nm)
            wt[k] = nb.astype(jnp.bfloat16)
            w_lo(k).start()
            w_core(k).start()
            mom[cols, at] = nm
            base[cols, at] = nb
            w_own(k).start()
            nm_own(k).start()
            nb_own(k).start()

        @pl.when(j >= SHIP + 3)
        def _():
            k = tile_of(j - (SHIP + 3))
            w_lo(k).wait_recv()
            w_fwd(k).start()

        return carry

    lax.fori_loop(0, SHIP + 3 + TILES, step, 0)

    for d in range(3):
        seg_x(d).wait_send()
        seg_z(d).wait_send()
    seg_help(far).wait_send()
    away(lambda: seg_native.wait_send())

    def drain(ref, sem):
        pltpu.make_async_copy(ref, ref, sem).wait()

    for sem in (a1s, b1s):
        drain(xg.at[0, :3], sem)
    for sem in (a2s, b2s):
        drain(xg.at[:2], sem)
    for sem in (a3s, b3s):
        drain(xg.at[:1], sem)
    drain(ysend.at[0], ys.at[0])
    away(lambda: drain(ysend.at[1], ys.at[1]))
    drain(xs, xss)
    drain(ps, pss)
    for u in (0, 1):
        pltpu.make_async_copy(cot.at[2 + u], cot.at[2 + u], cots.at[u]).wait()

        @pl.when(jnp.logical_not(at_home))
        def _():
            pltpu.make_async_copy(cot.at[2 + u], cot.at[2 + u], fwds.at[u]).wait()

    for sem in (wcs, wls, wfs, wcr, wfr, out_sem.at[0]):
        drain(wt, sem)
    drain(mom, out_sem.at[1])
    drain(base, out_sem.at[2])


def body(inputs, segments, cotangent, base, momentum):
    bf, f32, dma = jnp.bfloat16, jnp.float32, pltpu.SemaphoreType.DMA
    hbm = pl.BlockSpec(memory_space=pl.ANY)
    nb, nm, w = pl.pallas_call(
        kernel,
        out_shape=(
            jax.ShapeDtypeStruct((COLS, OWN), f32),
            jax.ShapeDtypeStruct((COLS, OWN), f32),
            jax.ShapeDtypeStruct((COLS, D), bf),
        ),
        in_specs=[pl.BlockSpec(memory_space=pltpu.VMEM), hbm, hbm, hbm, hbm],
        out_specs=(hbm, hbm, hbm),
        scratch_shapes=[
            pltpu.VMEM((STEPS, SIDE, SIDE, 2, TOK, 2 * BLOCK), bf),
            pltpu.VMEM((2, STEPS, TOK, 2 * BLOCK), bf),
            pltpu.VMEM((2, PART, TOK_G), bf),
            pltpu.VMEM((4, PART, TOK_G), bf),
            pltpu.VMEM((COLS, OWN), f32),
            pltpu.VMEM((COLS, OWN), f32),
            pltpu.VMEM((PART, 2 * BLOCK), f32),
            pltpu.VMEM((4, PART, BLOCK), f32),
            pltpu.VMEM((UNITS, PART, BLOCK), f32),
            pltpu.VMEM((UNITS, PART, BLOCK), f32),
            pltpu.VMEM((UNITS, PART, BLOCK), bf),
            pltpu.VMEM((TILES, 2, PART, BLOCK), bf),
            pltpu.VMEM((TILES, PART, BLOCK), bf),
            pltpu.VMEM((8, TOK), jnp.int32),
            pltpu.VMEM((SIDE, SIDE, 2, 8, TOK), jnp.int32),
            pltpu.VMEM((TOK_G // TOK, 8, TOK), f32),
            dma((4,)), dma((STEPS, 2, 2)), dma((3, 3)), dma((3, 3)),
            dma, dma((STEPS, 3)), dma, dma((STEPS, 2)), dma, dma((STEPS, 2)),
            dma, dma((STEPS, 3)), dma, dma((STEPS, 2)), dma, dma((STEPS, 2)),
            dma((2,)), dma((STEPS, 2)), dma((2,)), dma((2,)), dma((2, TOK_G // SWAP)), dma((2,)),
            dma, dma((UNITS,)), dma, dma((TILES, 2)),
            dma, dma, dma, dma((TILES,)), dma, dma, dma((3,)),
        ],
        compiler_params=pltpu.CompilerParams(
            collective_id=0, has_side_effects=True, vmem_limit_bytes=60 * 2**20
        ),
        cost_estimate=pl.CostEstimate(flops=2 * D * D * COLS, bytes_accessed=2**24, transcendentals=0),
    )(segments, inputs[0], cotangent[0].T, base.T, momentum.T)
    return nb.T, nm.T, w.T


def solution(mesh):
    return jax.shard_map(
        body,
        mesh=mesh,
        in_specs=(
            P("replica", "fsdp", None),
            P("replica", "fsdp"),
            P("replica", None, "fsdp"),
            P("replica", "fsdp"),
            P("replica", "fsdp"),
        ),
        out_specs=(P("replica", "fsdp"), P("replica", "fsdp"), P(None, "fsdp")),
        check_vma=False,
    )
```

```python
import jax
import jax.numpy as jnp
from jax import lax
from jax.experimental import pallas as pl
from jax.experimental.pallas import tpu as pltpu
from jax.sharding import PartitionSpec as P

D = 4096
BLOCK = 128
DOCS = 16
STEPS = 8
SIDE = 4
TOK = 128
TOK_G = 4096
COLS = 448
HALF = D // 2
OWN = D // 4
SWAP = 1024
PART = COLS // 2
TILES = 2 * STEPS
UNITS = 4 * STEPS
PASS = 3
DIRECT = 3
STORES = 4
SHIP = UNITS - TILES + 6
AHEAD = 3

inner_rate = 2.0
outer_rate = 0.7
nesterov_coef = 0.9
epsilon = 1e-06
MESH = pl.DeviceIdType.MESH


def kernel(
    seg_ref, inp_ref, cot_ref, base_ref, mom_ref,
    nb_out, nm_out, w_out,
    xg, ysend, raw, cot, base, mom, acc, keep, xs, xr, ps, rr, wt, seg_row, seg_own, segs, weight,
    load_sem, in_sem, seg_send, seg_recv,
    a1s, a1r, a2s, a2r, a3s, a3r, b1s, b1r, b2s, b2r, b3s, b3r, ys, yr, cots, cotr, rawr, fwds,
    xss, xsr, pss, psr, wcs, wcr, wls, wlr, wfs, wfr, out_sem,
):
    rep, f = lax.axis_index("replica"), lax.axis_index("fsdp")
    lo, core = rep // 2, rep % 2
    z, x, h = f // 8, (f // 2) % 4, f % 2

    def dev(x_=x, z_=z, h_=h, lo_=lo, core_=core):
        return (lo_ * 2 + core_, z_ * 8 + x_ * 2 + h_)

    def rot(v, d):
        return lax.rem(v + d, SIDE)

    other_core = dev(core_=1 - core)
    other_lo = dev(lo_=1 - lo)
    other_h = dev(h_=1 - h)
    across = dev(h_=1 - h, lo_=1 - lo)
    at_home = (h + core) % 2 == 0
    helper = dev(h_=jnp.where(at_home, 1 - h, h), lo_=1 - lo)
    other_both = dev(lo_=1 - lo, core_=1 - core)
    along_x = [dev(x_=rot(x, d)) for d in (1, 2, 3)]
    along_z = [dev(z_=rot(z, d)) for d in (1, 2, 3)]

    def remote(src, dst, ss, rs, to):
        return pltpu.make_async_remote_copy(
            src_ref=src, dst_ref=dst, send_sem=ss, recv_sem=rs, device_id=to, device_id_type=MESH
        )

    def lanes(at, size=BLOCK):
        return pl.ds(pl.multiple_of(at, BLOCK), size)

    barrier = pltpu.get_barrier_semaphore()
    partners = along_x + along_z + [other_core, other_lo, other_h, across, other_both]
    for to in partners:
        pl.semaphore_signal(barrier, inc=1, device_id=to, device_id_type=MESH)

    load_seg = pltpu.make_async_copy(seg_ref, seg_row, load_sem.at[4])
    load_seg.start()

    def load_rows(s, part, half, stay=False):
        hh = lo if half == 0 else 1 - lo
        dst = xg.at[s, z, x, h] if stay else ysend.at[half, s]
        return pltpu.make_async_copy(
            inp_ref.at[:, lanes(hh * HALF + part * OWN + s * BLOCK)],
            dst.at[:, part * BLOCK : (part + 1) * BLOCK],
            in_sem.at[s, part, half],
        )

    def load_all(s, carry):
        for part in (0, 1):
            load_rows(s, part, 0).start()

            @pl.when(at_home)
            def _():
                load_rows(s, part, 1, True).start()

            @pl.when(jnp.logical_not(at_home))
            def _():
                load_rows(s, part, 1).start()

        return carry

    lax.fori_loop(0, STEPS, load_all, 0)
    def load_cot(u):
        return pltpu.make_async_copy(cot_ref.at[u * PART : (u + 1) * PART], raw.at[u], load_sem.at[2 + u])

    load_base = pltpu.make_async_copy(base_ref, base, load_sem.at[0])
    load_mom = pltpu.make_async_copy(mom_ref, mom, load_sem.at[1])
    load_seg.wait()
    seg_own[...] = jnp.broadcast_to(seg_row[...], (8, TOK))

    @pl.when(at_home)
    def _():
        segs[z, x, h] = jnp.broadcast_to(seg_row[...], (8, TOK))

    pl.semaphore_wait(barrier, len(partners))

    far = jnp.where(at_home, 0, 1)

    def seg_help(kind):
        return remote(seg_own, segs.at[z, x, h], seg_send.at[2, 0], seg_recv.at[2, kind], helper)

    seg_native = remote(seg_own, segs.at[z, x, h], seg_send.at[2, 1], seg_recv.at[2, 0], other_h)

    def seg_x(d):
        return remote(segs.at[z, x], segs.at[z, x], seg_send.at[0, d], seg_recv.at[0, d], along_x[d])

    def seg_z(d):
        return remote(segs.at[z], segs.at[z], seg_send.at[1, d], seg_recv.at[1, d], along_z[d])

    def cross_help(s, kind):
        return remote(ysend.at[0, s], xg.at[s, z, x, h], ys.at[0], yr.at[s, kind], helper)

    def cross_native(s):
        return remote(ysend.at[1, s], xg.at[s, z, x, h], ys.at[1], yr.at[s, 0], other_h)

    def a1(s, d):
        ref = xg.at[s, z, x, h]
        return remote(ref, ref, a1s, a1r.at[s, d], along_x[d])

    def a2(s, d):
        ref = xg.at[s, z, :, h]
        return remote(ref, ref, a2s, a2r.at[s, d], along_z[2 * d])

    def a3(s, d):
        ref = xg.at[s, rot(z, 3 - 2 * d), 2 * d : 2 * d + 2, h]
        return remote(ref, ref, a3s, a3r.at[s, d], along_z[2 * d])

    def b1(s, d):
        ref = xg.at[s, z, x, 1 - h]
        return remote(ref, ref, b1s, b1r.at[s, d], along_z[d])

    def b2(s, d):
        ref = xg.at[s, :, x, 1 - h]
        return remote(ref, ref, b2s, b2r.at[s, d], along_x[2 * d])

    def b3(s, d):
        ref = xg.at[s, 2 * d : 2 * d + 2, rot(x, 3 - 2 * d), 1 - h]
        return remote(ref, ref, b3s, b3r.at[s, d], along_x[2 * d])

    def away(body):
        pl.when(jnp.logical_not(at_home))(body)

    seg_help(far).start()
    away(lambda: seg_native.start())

    def first(s, carry):
        for part in (0, 1):
            load_rows(s, part, 0).wait()
        cross_help(s, far).start()

        @pl.when(jnp.logical_not(at_home))
        def _():
            for part in (0, 1):
                load_rows(s, part, 1).wait()
            cross_native(s).start()

        return carry

    def start_own(s):
        @pl.when(at_home)
        def _():
            for part in (0, 1):
                load_rows(s, part, 1, True).wait()

        @pl.when(jnp.logical_not(at_home))
        def _():
            cross_help(s, 1).wait_recv()

        for d in range(3):
            a1(s, d).start()

    def partner1(s):
        cross_help(s, 0).wait_recv()
        for d in range(3):
            b1(s, d).start()

    def tick(i):
        def at(s, body):
            @pl.when((s >= 0) & (s < STEPS))
            def _():
                body(s)

        def own2(s):
            for d in range(3):
                a1(s, d).wait_recv()
            for d in range(2):
                a2(s, d).start()

        def own3(s):
            for d in range(2):
                a2(s, d).wait_recv()
            for d in range(2):
                a3(s, d).start()

        def partner2(s):
            for d in range(3):
                b1(s, d).wait_recv()
            for d in range(2):
                b2(s, d).start()

        def partner3(s):
            for d in range(2):
                b2(s, d).wait_recv()
            for d in range(2):
                b3(s, d).start()

        at(i - 2, own3)
        at(i - 2, partner3)
        at(i - 1, own2)
        at(i - 1, partner2)
        at(i + 1, partner1)
        at(i + 3, start_own)

    def send_cot(u):
        @pl.when(at_home)
        def _():
            def go(i, carry):
                at = lanes(i * SWAP, SWAP)
                remote(cot_ref.at[u * PART : (u + 1) * PART, at], cot.at[2 + u, :, at], cots.at[u], cotr.at[u], across).start()
                return carry

            lax.fori_loop(0, TOK_G // SWAP, go, 0)

        @pl.when(jnp.logical_not(at_home))
        def _():
            def go(i, carry):
                at = lanes(i * SWAP, SWAP)
                remote(cot_ref.at[u * PART : (u + 1) * PART, at], raw.at[u, :, at], cots.at[u], rawr.at[u, i], other_lo).start()
                return carry

            lax.fori_loop(0, TOK_G // SWAP, go, 0)

    def pass_cot(u, first, last):
        @pl.when(jnp.logical_not(at_home))
        def _():
            def go(i, carry):
                at = lanes(i * SWAP, SWAP)
                remote(raw.at[u, :, at], raw.at[u, :, at], cots.at[u], rawr.at[u, i], other_lo).wait_recv()
                remote(raw.at[u, :, at], cot.at[2 + u, :, at], fwds.at[u], cotr.at[u], across).start()
                return carry

            lax.fori_loop(first, last, go, 0)

    lax.fori_loop(0, STEPS, first, 0)
    send_cot(0)
    send_cot(1)
    start_own(0)
    partner1(0)
    start_own(1)
    start_own(2)
    seg_help(0).wait_recv()
    away(lambda: seg_help(1).wait_recv())
    for d in range(3):
        seg_x(d).start()
    tick(0)

    @pl.when(at_home)
    def _():
        load_cot(0).start()
        load_cot(1).start()

    load_base.start()
    load_mom.start()
    for d in range(3):
        seg_x(d).wait_recv()
    for d in range(3):
        seg_z(d).start()
    tick(1)
    tick(2)
    for d in range(3):
        seg_z(d).wait_recv()
    pass_cot(0, 0, 2)
    tick(3)
    pass_cot(0, 2, TOK_G // SWAP)

    ids = segs[...].reshape(TOK_G // TOK, 8, TOK)
    per_token = jnp.zeros((TOK_G // TOK, 8, TOK), jnp.float32)
    for doc in range(DOCS):
        mine = (ids == doc).astype(jnp.float32)
        count = jnp.sum(jnp.sum(mine, axis=0), axis=1, keepdims=True)
        per_token = per_token + mine * (1.0 / count)[None]
    weight[...] = per_token

    def scale_cot(src, g):
        def tile(i, carry):
            at = lanes(i * TOK)
            block = src[:, at].astype(jnp.float32).reshape(PART // 8, 8, TOK)
            cot[g, :, at] = (block * weight[i][None]).reshape(PART, TOK).astype(jnp.bfloat16)
            return carry

        lax.fori_loop(0, TOK_G // TOK, tile, 0)

    def scale_own(u):
        @pl.when(at_home)
        def _():
            load_cot(u).wait()

        scale_cot(raw.at[u], u)

    scale_own(0)

    def swap(j):
        return remote(xs.at[j], xr.at[j], xss, xsr.at[j], other_core)

    def to_owner(j, g, s):
        k, side = (g % 2) * STEPS + s, g // 2
        return remote(ps.at[j], rr.at[k, side], pss, psr.at[k, side], dev(h_=jnp.where(g < 2, h, 1 - h), lo_=1 - lo))

    def from_owner(k, side):
        return remote(ps.at[0], rr.at[k, side], pss, psr.at[k, side], other_lo)

    def place(k, ref, rp=None):
        u, s = k // STEPS, k % STEPS
        first = s * BLOCK if rp is None else rp * OWN + s * BLOCK
        return ref.at[pl.ds(pl.multiple_of(u * PART, 32), PART), lanes(first)]

    def w_core(k):
        return remote(wt.at[k], place(k, w_out, rep), wcs, wcr, other_core)

    def w_lo(k):
        return remote(wt.at[k], place(k, w_out, rep), wls, wlr.at[k], other_lo)

    def w_fwd(k):
        there = place(k, w_out, (1 - lo) * 2 + core)
        return remote(there, there, wfs, wfr, other_core)

    def w_diag(k):
        return remote(wt.at[k], place(k, w_out, rep), wfs, wfr, other_both)

    def w_own(k):
        return pltpu.make_async_copy(wt.at[k], place(k, w_out, rep), out_sem.at[0])

    def nm_own(k):
        return pltpu.make_async_copy(place(k, mom), place(k, nm_out), out_sem.at[1])

    def nb_own(k):
        return pltpu.make_async_copy(place(k, base), place(k, nb_out), out_sem.at[2])

    def quantized(at):
        blk = inner_rate * acc[:, lanes(at * BLOCK)]
        scale = (jnp.max(jnp.abs(blk), axis=1, keepdims=True) + epsilon).astype(jnp.bfloat16)
        scale = scale.astype(jnp.float32)
        coded = (blk * (1.0 / scale)).astype(jnp.bfloat16)
        return coded.astype(jnp.float32) * scale

    def pick(j, *cases):
        value = cases[-1]
        for bound, case in reversed(cases[:-1]):
            value = jnp.where(j < bound, case, value)
        return value

    def unit(j):
        g = pick(j, (6, j // 3), (10, j % 2), (15, 2), (21, j % 3), (28, 3), (31, j - 28), 3)
        s = pick(j, (6, j % 3), (10, j // 2), (15, j - 10), (21, j // 3), (28, j - 21), STEPS - 1)
        return g, s

    def tile_of(m):
        return pick(m, (7, m), (14, m + 1), (15, 7), m)

    def step(j, carry):
        @pl.when(j < UNITS)
        def _():
            g, s = unit(j)

            @pl.when(g == 0)
            def _():
                for d in range(2):
                    a3(s, d).wait_recv()
                    b3(s, d).wait_recv()

            @pl.when(j == 3)
            def _():
                pass_cot(1, 0, TOK_G // SWAP)
                scale_own(1)

            for u, at in ((0, 10), (1, 21)):

                @pl.when(j == at)
                def _():
                    got = cot.at[2 + u]
                    pltpu.make_async_copy(got, got, cotr.at[u]).wait()
                    scale_cot(got, 2 + u)

            acc[...] = jnp.dot(cot[g], xg[s].reshape(TOK_G, 2 * BLOCK), preferred_element_type=jnp.float32)
            xs[j] = quantized(1 - core)
            swap(j).start()
            keep[j % 4] = quantized(core)

            @pl.when(((g == 0) & (s > 0) & (s < 3)) | ((g == 1) & (s >= 3)))
            def _():
                tick(s + AHEAD)

        @pl.when((j >= PASS) & (j < UNITS + PASS))
        def _():
            q = j - PASS
            g, s = unit(q)
            swap(q).wait_recv()
            ps[q] = (keep[q % 4] + xr[q]).astype(jnp.bfloat16)
            to_owner(q, g, s).start()

        @pl.when(j == SHIP)
        def _():
            load_base.wait()
            load_mom.wait()

        @pl.when((j >= SHIP) & (j < SHIP + TILES))
        def _():
            k = tile_of(j - SHIP)
            from_owner(k, 0).wait_recv()
            from_owner(k, 1).wait_recv()
            average = (rr[k, 0].astype(jnp.float32) + rr[k, 1].astype(jnp.float32)) * 0.25
            u, s = k // STEPS, k % STEPS
            cols, at = pl.ds(pl.multiple_of(u * PART, 32), PART), lanes(s * BLOCK)
            nm = nesterov_coef * mom[cols, at] + average
            nb = base[cols, at] - outer_rate * (average + nesterov_coef * nm)
            wt[k] = nb.astype(jnp.bfloat16)
            w_lo(k).start()

            @pl.when(j >= SHIP + TILES - DIRECT)
            def _():
                w_diag(k).start()

            w_core(k).start()
            mom[cols, at] = nm
            base[cols, at] = nb
            w_own(k).start()
            nm_own(k).start()
            nb_own(k).start()

        @pl.when((j >= SHIP + 3) & (j < SHIP + 3 + TILES - DIRECT))
        def _():
            k = tile_of(j - (SHIP + 3))
            w_lo(k).wait_recv()
            w_fwd(k).start()

        return carry

    lax.fori_loop(0, SHIP + TILES, step, 0)

    for d in range(3):
        seg_x(d).wait_send()
        seg_z(d).wait_send()
    seg_help(far).wait_send()
    away(lambda: seg_native.wait_send())

    def drain(ref, sem):
        pltpu.make_async_copy(ref, ref, sem).wait()

    for sem in (a1s, b1s):
        drain(xg.at[0, :3], sem)
    for sem in (a2s, b2s):
        drain(xg.at[:2], sem)
    for sem in (a3s, b3s):
        drain(xg.at[:1], sem)
    drain(ysend.at[0], ys.at[0])
    away(lambda: drain(ysend.at[1], ys.at[1]))
    drain(xs, xss)
    drain(ps, pss)
    for u in (0, 1):
        pltpu.make_async_copy(cot.at[2 + u], cot.at[2 + u], cots.at[u]).wait()

        @pl.when(jnp.logical_not(at_home))
        def _():
            pltpu.make_async_copy(cot.at[2 + u], cot.at[2 + u], fwds.at[u]).wait()

    for sem in (wcs, wls, wfs, wcr, wfr, out_sem.at[0]):
        drain(wt, sem)
    for m in range(TILES - DIRECT, TILES):
        w_lo(tile_of(m)).wait_recv()
    drain(mom, out_sem.at[1])
    drain(base, out_sem.at[2])


def store(nb, nm, w, nb_out, nm_out, w_out):
    nb_out[...] = nb[...]
    nm_out[...] = nm[...]
    w_out[...] = w[...]


def body(inputs, segments, cotangent, base, momentum):
    bf, f32, dma = jnp.bfloat16, jnp.float32, pltpu.SemaphoreType.DMA
    hbm = pl.BlockSpec(memory_space=pl.ANY)
    nb, nm, w = pl.pallas_call(
        kernel,
        out_shape=(
            jax.ShapeDtypeStruct((COLS, OWN), f32),
            jax.ShapeDtypeStruct((COLS, OWN), f32),
            jax.ShapeDtypeStruct((COLS, D), bf),
        ),
        in_specs=[hbm] * 5,
        out_specs=(hbm, hbm, hbm),
        scratch_shapes=[
            pltpu.VMEM((STEPS, SIDE, SIDE, 2, TOK, 2 * BLOCK), bf),
            pltpu.VMEM((2, STEPS, TOK, 2 * BLOCK), bf),
            pltpu.VMEM((2, PART, TOK_G), bf),
            pltpu.VMEM((4, PART, TOK_G), bf),
            pltpu.VMEM((COLS, OWN), f32),
            pltpu.VMEM((COLS, OWN), f32),
            pltpu.VMEM((PART, 2 * BLOCK), f32),
            pltpu.VMEM((4, PART, BLOCK), f32),
            pltpu.VMEM((UNITS, PART, BLOCK), f32),
            pltpu.VMEM((UNITS, PART, BLOCK), f32),
            pltpu.VMEM((UNITS, PART, BLOCK), bf),
            pltpu.VMEM((TILES, 2, PART, BLOCK), bf),
            pltpu.VMEM((TILES, PART, BLOCK), bf),
            pltpu.VMEM((1, TOK), jnp.int32),
            pltpu.VMEM((8, TOK), jnp.int32),
            pltpu.VMEM((SIDE, SIDE, 2, 8, TOK), jnp.int32),
            pltpu.VMEM((TOK_G // TOK, 8, TOK), f32),
            dma((5,)), dma((STEPS, 2, 2)), dma((3, 3)), dma((3, 3)),
            dma, dma((STEPS, 3)), dma, dma((STEPS, 2)), dma, dma((STEPS, 2)),
            dma, dma((STEPS, 3)), dma, dma((STEPS, 2)), dma, dma((STEPS, 2)),
            dma((2,)), dma((STEPS, 2)), dma((2,)), dma((2,)), dma((2, TOK_G // SWAP)), dma((2,)),
            dma, dma((UNITS,)), dma, dma((TILES, 2)),
            dma, dma, dma, dma((TILES,)), dma, dma, dma((3,)),
        ],
        compiler_params=pltpu.CompilerParams(
            collective_id=0, has_side_effects=True, vmem_limit_bytes=60 * 2**20
        ),
        cost_estimate=pl.CostEstimate(flops=2 * D * D * COLS, bytes_accessed=2**24, transcendentals=0),
    )(segments, inputs[0], cotangent[0].T, base.T, momentum.T)
    nb, nm, w = pl.pallas_call(
        store,
        out_shape=(
            jax.ShapeDtypeStruct((COLS, OWN), f32),
            jax.ShapeDtypeStruct((COLS, OWN), f32),
            jax.ShapeDtypeStruct((COLS, D), bf),
        ),
        grid=(STORES,),
        in_specs=[pl.BlockSpec((COLS // STORES, width), lambda i: (i, 0)) for width in (OWN, OWN, D)],
        out_specs=tuple(pl.BlockSpec((COLS // STORES, width), lambda i: (i, 0)) for width in (OWN, OWN, D)),
    )(nb, nm, w)
    return nb.T, nm.T, w.T


def solution(mesh):
    return jax.shard_map(
        body,
        mesh=mesh,
        in_specs=(
            P("replica", "fsdp", None),
            P("replica", "fsdp"),
            P("replica", None, "fsdp"),
            P("replica", "fsdp"),
            P("replica", "fsdp"),
        ),
        out_specs=(P("replica", "fsdp"), P("replica", "fsdp"), P(None, "fsdp")),
        check_vma=False,
    )
```

```python
import jax
import jax.numpy as jnp
from jax import lax
from jax.experimental import pallas as pl
from jax.experimental.pallas import tpu as pltpu
from jax.sharding import PartitionSpec as P

D = 4096
BLOCK = 128
DOCS = 16
STEPS = 8
SIDE = 4
TOK = 128
TOK_G = 4096
COLS = 448
HALF = D // 2
OWN = D // 4
SWAP = 1024
PART = COLS // 2
TILES = 2 * STEPS
UNITS = 4 * STEPS
PASS = 1
FWD = 3
DIRECT = 1
STORES = 4
SHIP = UNITS - TILES + 2
AHEAD = 3
RELAYED = STEPS - 1

inner_rate = 2.0
outer_rate = 0.7
nesterov_coef = 0.9
epsilon = 1e-06
MESH = pl.DeviceIdType.MESH


def kernel(
    seg_ref, inp_ref, cot_ref, base_ref, mom_ref,
    nb_out, nm_out, w_out,
    xg, ysend, raw, cot, base, mom, acc, keep, xs, xr, ps, rr, wt, seg_row, seg_own, segs, weight,
    load_sem, in_sem, seg_send, seg_recv,
    a1s, a1r, a2s, a2r, a3s, a3r, b1s, b1r, b2s, b2r, b3s, b3r, ys, yr, cots, cotr, rawr, fwds,
    xss, xsr, pss, psr, wcs, wcr, wls, wlr, wfs, wfr, out_sem,
):
    rep, f = lax.axis_index("replica"), lax.axis_index("fsdp")
    lo, core = rep // 2, rep % 2
    z, x, h = f // 8, (f // 2) % 4, f % 2

    def dev(x_=x, z_=z, h_=h, lo_=lo, core_=core):
        return (lo_ * 2 + core_, z_ * 8 + x_ * 2 + h_)

    def rot(v, d):
        return lax.rem(v + d, SIDE)

    other_core = dev(core_=1 - core)
    other_lo = dev(lo_=1 - lo)
    other_h = dev(h_=1 - h)
    across = dev(h_=1 - h, lo_=1 - lo)
    at_home = (h + core) % 2 == 0
    helper = dev(h_=jnp.where(at_home, 1 - h, h), lo_=1 - lo)
    other_both = dev(lo_=1 - lo, core_=1 - core)
    along_x = [dev(x_=rot(x, d)) for d in (1, 2, 3)]
    along_z = [dev(z_=rot(z, d)) for d in (1, 2, 3)]

    def remote(src, dst, ss, rs, to):
        return pltpu.make_async_remote_copy(
            src_ref=src, dst_ref=dst, send_sem=ss, recv_sem=rs, device_id=to, device_id_type=MESH
        )

    def lanes(at, size=BLOCK):
        return pl.ds(pl.multiple_of(at, BLOCK), size)

    barrier = pltpu.get_barrier_semaphore()
    partners = along_x + along_z + [other_core, other_lo, other_h, across, other_both]
    for to in partners:
        pl.semaphore_signal(barrier, inc=1, device_id=to, device_id_type=MESH)

    load_seg = pltpu.make_async_copy(seg_ref, seg_row, load_sem.at[4])
    load_seg.start()

    def load_rows(s, part, half, stay=False):
        hh = lo if half == 0 else 1 - lo
        dst = xg.at[s, z, x, h] if stay else ysend.at[half, s]
        return pltpu.make_async_copy(
            inp_ref.at[:, lanes(hh * HALF + part * OWN + s * BLOCK)],
            dst.at[:, part * BLOCK : (part + 1) * BLOCK],
            in_sem.at[s, part, half],
        )

    def load_all(s, carry):
        for part in (0, 1):
            load_rows(s, part, 0).start()

            @pl.when(at_home)
            def _():
                load_rows(s, part, 1, True).start()

            @pl.when(jnp.logical_not(at_home))
            def _():
                load_rows(s, part, 1).start()

        return carry

    lax.fori_loop(0, STEPS, load_all, 0)
    def load_cot(u):
        return pltpu.make_async_copy(cot_ref.at[u * PART : (u + 1) * PART], raw.at[u], load_sem.at[2 + u])

    load_base = pltpu.make_async_copy(base_ref, base, load_sem.at[0])
    load_mom = pltpu.make_async_copy(mom_ref, mom, load_sem.at[1])
    load_seg.wait()
    seg_own[...] = jnp.broadcast_to(seg_row[...], (8, TOK))

    @pl.when(at_home)
    def _():
        segs[z, x, h] = jnp.broadcast_to(seg_row[...], (8, TOK))

    pl.semaphore_wait(barrier, len(partners))

    far = jnp.where(at_home, 0, 1)

    def seg_help(kind):
        return remote(seg_own, segs.at[z, x, h], seg_send.at[2, 0], seg_recv.at[2, kind], helper)

    seg_native = remote(seg_own, segs.at[z, x, h], seg_send.at[2, 1], seg_recv.at[2, 0], other_h)

    def seg_x(d):
        return remote(segs.at[z, x], segs.at[z, x], seg_send.at[0, d], seg_recv.at[0, d], along_x[d])

    def seg_z(d):
        return remote(segs.at[z], segs.at[z], seg_send.at[1, d], seg_recv.at[1, d], along_z[d])

    def cross_help(s, kind):
        return remote(ysend.at[0, s], xg.at[s, z, x, h], ys.at[0], yr.at[s, kind], helper)

    def cross_native(s):
        return remote(ysend.at[1, s], xg.at[s, z, x, h], ys.at[1], yr.at[s, 0], other_h)

    def a1(s, d):
        ref = xg.at[s, z, x, h]
        return remote(ref, ref, a1s, a1r.at[s, d], along_x[d])

    def a2(s, d):
        ref = xg.at[s, z, :, h]
        return remote(ref, ref, a2s, a2r.at[s, d], along_z[2 * d])

    def a3(s, d):
        ref = xg.at[s, rot(z, 3 - 2 * d), 2 * d : 2 * d + 2, h]
        return remote(ref, ref, a3s, a3r.at[s, d], along_z[2 * d])

    def a_far(s):
        ref = xg.at[s, z, :, h]
        return remote(ref, ref, a3s, a3r.at[s, 0], along_z[1])

    def b_far(s):
        ref = xg.at[s, :, x, 1 - h]
        return remote(ref, ref, b3s, b3r.at[s, 0], along_x[1])

    def b1(s, d):
        ref = xg.at[s, z, x, 1 - h]
        return remote(ref, ref, b1s, b1r.at[s, d], along_z[d])

    def b2(s, d):
        ref = xg.at[s, :, x, 1 - h]
        return remote(ref, ref, b2s, b2r.at[s, d], along_x[2 * d])

    def b3(s, d):
        ref = xg.at[s, 2 * d : 2 * d + 2, rot(x, 3 - 2 * d), 1 - h]
        return remote(ref, ref, b3s, b3r.at[s, d], along_x[2 * d])

    def away(body):
        pl.when(jnp.logical_not(at_home))(body)

    seg_help(far).start()
    away(lambda: seg_native.start())

    def first(s, carry):
        for part in (0, 1):
            load_rows(s, part, 0).wait()
        cross_help(s, far).start()

        @pl.when(jnp.logical_not(at_home))
        def _():
            for part in (0, 1):
                load_rows(s, part, 1).wait()
            cross_native(s).start()

        return carry

    def start_own(s):
        @pl.when(at_home)
        def _():
            for part in (0, 1):
                load_rows(s, part, 1, True).wait()

        @pl.when(jnp.logical_not(at_home))
        def _():
            cross_help(s, 1).wait_recv()

        for d in range(3):
            a1(s, d).start()

    def partner1(s):
        cross_help(s, 0).wait_recv()
        for d in range(3):
            b1(s, d).start()

    def tick(i):
        def at(s, body, end=STEPS):
            @pl.when((s >= 0) & (s < end))
            def _():
                body(s)

        def own2(s):
            for d in range(3):
                a1(s, d).wait_recv()
            for d in range(2):
                a2(s, d).start()

            @pl.when(s >= RELAYED)
            def _():
                a_far(s).start()

        def own3(s):
            for d in range(2):
                a2(s, d).wait_recv()
            for d in range(2):
                a3(s, d).start()

        def partner2(s):
            for d in range(3):
                b1(s, d).wait_recv()
            for d in range(2):
                b2(s, d).start()

            @pl.when(s >= RELAYED)
            def _():
                b_far(s).start()

        def partner3(s):
            for d in range(2):
                b2(s, d).wait_recv()
            for d in range(2):
                b3(s, d).start()

        at(i - 2, own3, RELAYED)
        at(i - 2, partner3, RELAYED)
        at(i - 1, own2)
        at(i - 1, partner2)
        at(i + 1, partner1)
        at(i + 3, start_own)

    def send_cot(u):
        @pl.when(at_home)
        def _():
            def go(i, carry):
                at = lanes(i * SWAP, SWAP)
                remote(cot_ref.at[u * PART : (u + 1) * PART, at], cot.at[2 + u, :, at], cots.at[u], cotr.at[u], across).start()
                return carry

            lax.fori_loop(0, TOK_G // SWAP, go, 0)

        @pl.when(jnp.logical_not(at_home))
        def _():
            def go(i, carry):
                at = lanes(i * SWAP, SWAP)
                remote(cot_ref.at[u * PART : (u + 1) * PART, at], raw.at[u, :, at], cots.at[u], rawr.at[u, i], other_lo).start()
                return carry

            lax.fori_loop(0, TOK_G // SWAP, go, 0)

    def pass_cot(u, first, last):
        @pl.when(jnp.logical_not(at_home))
        def _():
            def go(i, carry):
                at = lanes(i * SWAP, SWAP)
                remote(raw.at[u, :, at], raw.at[u, :, at], cots.at[u], rawr.at[u, i], other_lo).wait_recv()
                remote(raw.at[u, :, at], cot.at[2 + u, :, at], fwds.at[u], cotr.at[u], across).start()
                return carry

            lax.fori_loop(first, last, go, 0)

    lax.fori_loop(0, STEPS, first, 0)
    send_cot(0)
    send_cot(1)
    start_own(0)
    partner1(0)
    start_own(1)
    start_own(2)
    seg_help(0).wait_recv()
    away(lambda: seg_help(1).wait_recv())
    for d in range(3):
        seg_x(d).start()
    tick(0)

    @pl.when(at_home)
    def _():
        load_cot(0).start()
        load_cot(1).start()

    load_base.start()
    load_mom.start()
    for d in range(3):
        seg_x(d).wait_recv()
    for d in range(3):
        seg_z(d).start()
    tick(1)
    tick(2)
    for d in range(3):
        seg_z(d).wait_recv()
    pass_cot(0, 0, 2)
    tick(3)
    pass_cot(0, 2, TOK_G // SWAP)

    ids = segs[...].reshape(TOK_G // TOK, 8, TOK)
    per_token = jnp.zeros((TOK_G // TOK, 8, TOK), jnp.float32)
    for doc in range(DOCS):
        mine = (ids == doc).astype(jnp.float32)
        count = jnp.sum(jnp.sum(mine, axis=0), axis=1, keepdims=True)
        per_token = per_token + mine * (1.0 / count)[None]
    weight[...] = per_token

    def scale_cot(src, g):
        def tile(i, carry):
            at = lanes(i * TOK)
            block = src[:, at].astype(jnp.float32).reshape(PART // 8, 8, TOK)
            cot[g, :, at] = (block * weight[i][None]).reshape(PART, TOK).astype(jnp.bfloat16)
            return carry

        lax.fori_loop(0, TOK_G // TOK, tile, 0)

    def scale_own(u):
        @pl.when(at_home)
        def _():
            load_cot(u).wait()

        scale_cot(raw.at[u], u)

    scale_own(0)

    def swap(j):
        return remote(xs.at[j], xr.at[j], xss, xsr.at[j], other_core)

    def to_owner(j, g, s):
        k, side = (g % 2) * STEPS + s, g // 2
        return remote(ps.at[j], rr.at[k, side], pss, psr.at[k, side], dev(h_=jnp.where(g < 2, h, 1 - h), lo_=1 - lo))

    def from_owner(k, side):
        return remote(ps.at[0], rr.at[k, side], pss, psr.at[k, side], other_lo)

    def place(k, ref, rp=None):
        u, s = k // STEPS, k % STEPS
        first = s * BLOCK if rp is None else rp * OWN + s * BLOCK
        return ref.at[pl.ds(pl.multiple_of(u * PART, 32), PART), lanes(first)]

    def w_core(k):
        return remote(wt.at[k], place(k, w_out, rep), wcs, wcr, other_core)

    def w_lo(k):
        return remote(wt.at[k], place(k, w_out, rep), wls, wlr.at[k], other_lo)

    def w_fwd(k):
        there = place(k, w_out, (1 - lo) * 2 + core)
        return remote(there, there, wfs, wfr, other_core)

    def w_diag(k):
        return remote(wt.at[k], place(k, w_out, rep), wfs, wfr, other_both)

    def w_own(k):
        return pltpu.make_async_copy(wt.at[k], place(k, w_out, rep), out_sem.at[0])

    def nm_own(k):
        return pltpu.make_async_copy(place(k, mom), place(k, nm_out), out_sem.at[1])

    def nb_own(k):
        return pltpu.make_async_copy(place(k, base), place(k, nb_out), out_sem.at[2])

    def quantized(at):
        blk = inner_rate * acc[:, lanes(at * BLOCK)]
        scale = (jnp.max(jnp.abs(blk), axis=1, keepdims=True) + epsilon).astype(jnp.bfloat16)
        scale = scale.astype(jnp.float32)
        coded = (blk * (1.0 / scale)).astype(jnp.bfloat16)
        return coded.astype(jnp.float32) * scale

    def pick(j, *cases):
        value = cases[-1]
        for bound, case in reversed(cases[:-1]):
            value = jnp.where(j < bound, case, value)
        return value

    def unit(j):
        g = pick(j, (6, j // 3), (10, j % 2), (15, 2), (21, j % 3), (28, 3), (31, j - 28), 3)
        s = pick(j, (6, j % 3), (10, j // 2), (15, j - 10), (21, j // 3), (28, j - 21), STEPS - 1)
        return g, s

    def tile_of(m):
        return pick(m, (7, m), (14, m + 1), (15, 7), m)

    def step(j, carry):
        @pl.when(j < UNITS)
        def _():
            g, s = unit(j)

            @pl.when(g == 0)
            def _():
                @pl.when(s < RELAYED)
                def _():
                    for d in range(2):
                        a3(s, d).wait_recv()
                        b3(s, d).wait_recv()

                @pl.when(s >= RELAYED)
                def _():
                    for d in range(2):
                        a2(s, d).wait_recv()
                        b2(s, d).wait_recv()
                    a_far(s).wait_recv()
                    b_far(s).wait_recv()

            @pl.when(j == 3)
            def _():
                pass_cot(1, 0, TOK_G // SWAP)
                scale_own(1)

            for u, at in ((0, 10), (1, 21)):

                @pl.when(j == at)
                def _():
                    got = cot.at[2 + u]
                    pltpu.make_async_copy(got, got, cotr.at[u]).wait()
                    scale_cot(got, 2 + u)

            acc[...] = jnp.dot(cot[g], xg[s].reshape(TOK_G, 2 * BLOCK), preferred_element_type=jnp.float32)
            xs[j] = quantized(1 - core)
            swap(j).start()
            keep[j % 4] = quantized(core)

            @pl.when(((g == 0) & (s > 0) & (s < 3)) | ((g == 1) & (s >= 3)))
            def _():
                tick(s + AHEAD)

        @pl.when((j >= PASS) & (j < UNITS + PASS))
        def _():
            q = j - PASS
            g, s = unit(q)
            swap(q).wait_recv()
            ps[q] = (keep[q % 4] + xr[q]).astype(jnp.bfloat16)
            to_owner(q, g, s).start()

        @pl.when(j == SHIP)
        def _():
            load_base.wait()
            load_mom.wait()

        @pl.when((j >= SHIP) & (j < SHIP + TILES))
        def _():
            k = tile_of(j - SHIP)
            from_owner(k, 0).wait_recv()
            from_owner(k, 1).wait_recv()
            average = (rr[k, 0].astype(jnp.float32) + rr[k, 1].astype(jnp.float32)) * 0.25
            u, s = k // STEPS, k % STEPS
            cols, at = pl.ds(pl.multiple_of(u * PART, 32), PART), lanes(s * BLOCK)
            nm = nesterov_coef * mom[cols, at] + average
            nb = base[cols, at] - outer_rate * (average + nesterov_coef * nm)
            wt[k] = nb.astype(jnp.bfloat16)
            w_lo(k).start()

            @pl.when(j >= SHIP + TILES - DIRECT)
            def _():
                w_diag(k).start()

            w_core(k).start()
            mom[cols, at] = nm
            base[cols, at] = nb
            w_own(k).start()
            nm_own(k).start()
            nb_own(k).start()

        @pl.when((j >= SHIP + FWD) & (j < SHIP + FWD + TILES - DIRECT))
        def _():
            k = tile_of(j - (SHIP + FWD))
            w_lo(k).wait_recv()
            w_fwd(k).start()

        return carry

    lax.fori_loop(0, SHIP + TILES + max(0, FWD - DIRECT), step, 0)

    for d in range(3):
        seg_x(d).wait_send()
        seg_z(d).wait_send()
    seg_help(far).wait_send()
    away(lambda: seg_native.wait_send())

    def drain(ref, sem):
        pltpu.make_async_copy(ref, ref, sem).wait()

    for sem in (a1s, b1s):
        drain(xg.at[0, :3], sem)
    for sem in (a2s, b2s):
        drain(xg.at[:2], sem)
    for sem in (a3s, b3s):
        drain(xg.at[:1], sem)
    drain(ysend.at[0], ys.at[0])
    away(lambda: drain(ysend.at[1], ys.at[1]))
    drain(xs, xss)
    drain(ps, pss)
    for u in (0, 1):
        pltpu.make_async_copy(cot.at[2 + u], cot.at[2 + u], cots.at[u]).wait()

        @pl.when(jnp.logical_not(at_home))
        def _():
            pltpu.make_async_copy(cot.at[2 + u], cot.at[2 + u], fwds.at[u]).wait()

    for sem in (wcs, wls, wfs, wcr, wfr, out_sem.at[0]):
        drain(wt, sem)
    for m in range(TILES - DIRECT, TILES):
        w_lo(tile_of(m)).wait_recv()
    drain(mom, out_sem.at[1])
    drain(base, out_sem.at[2])


def store(nb, nm, w, nb_out, nm_out, w_out):
    nb_out[...] = nb[...]
    nm_out[...] = nm[...]
    w_out[...] = w[...]


def body(inputs, segments, cotangent, base, momentum):
    bf, f32, dma = jnp.bfloat16, jnp.float32, pltpu.SemaphoreType.DMA
    hbm = pl.BlockSpec(memory_space=pl.ANY)
    nb, nm, w = pl.pallas_call(
        kernel,
        out_shape=(
            jax.ShapeDtypeStruct((COLS, OWN), f32),
            jax.ShapeDtypeStruct((COLS, OWN), f32),
            jax.ShapeDtypeStruct((COLS, D), bf),
        ),
        in_specs=[hbm] * 5,
        out_specs=(hbm, hbm, hbm),
        scratch_shapes=[
            pltpu.VMEM((STEPS, SIDE, SIDE, 2, TOK, 2 * BLOCK), bf),
            pltpu.VMEM((2, STEPS, TOK, 2 * BLOCK), bf),
            pltpu.VMEM((2, PART, TOK_G), bf),
            pltpu.VMEM((4, PART, TOK_G), bf),
            pltpu.VMEM((COLS, OWN), f32),
            pltpu.VMEM((COLS, OWN), f32),
            pltpu.VMEM((PART, 2 * BLOCK), f32),
            pltpu.VMEM((4, PART, BLOCK), f32),
            pltpu.VMEM((UNITS, PART, BLOCK), f32),
            pltpu.VMEM((UNITS, PART, BLOCK), f32),
            pltpu.VMEM((UNITS, PART, BLOCK), bf),
            pltpu.VMEM((TILES, 2, PART, BLOCK), bf),
            pltpu.VMEM((TILES, PART, BLOCK), bf),
            pltpu.VMEM((1, TOK), jnp.int32),
            pltpu.VMEM((8, TOK), jnp.int32),
            pltpu.VMEM((SIDE, SIDE, 2, 8, TOK), jnp.int32),
            pltpu.VMEM((TOK_G // TOK, 8, TOK), f32),
            dma((5,)), dma((STEPS, 2, 2)), dma((3, 3)), dma((3, 3)),
            dma, dma((STEPS, 3)), dma, dma((STEPS, 2)), dma, dma((STEPS, 2)),
            dma, dma((STEPS, 3)), dma, dma((STEPS, 2)), dma, dma((STEPS, 2)),
            dma((2,)), dma((STEPS, 2)), dma((2,)), dma((2,)), dma((2, TOK_G // SWAP)), dma((2,)),
            dma, dma((UNITS,)), dma, dma((TILES, 2)),
            dma, dma, dma, dma((TILES,)), dma, dma, dma((3,)),
        ],
        compiler_params=pltpu.CompilerParams(
            collective_id=0, has_side_effects=True, vmem_limit_bytes=60 * 2**20
        ),
        cost_estimate=pl.CostEstimate(flops=2 * D * D * COLS, bytes_accessed=2**24, transcendentals=0),
    )(segments, inputs[0], cotangent[0].T, base.T, momentum.T)
    nb, nm, w = pl.pallas_call(
        store,
        out_shape=(
            jax.ShapeDtypeStruct((COLS, OWN), f32),
            jax.ShapeDtypeStruct((COLS, OWN), f32),
            jax.ShapeDtypeStruct((COLS, D), bf),
        ),
        grid=(STORES,),
        in_specs=[pl.BlockSpec((COLS // STORES, width), lambda i: (i, 0)) for width in (OWN, OWN, D)],
        out_specs=tuple(pl.BlockSpec((COLS // STORES, width), lambda i: (i, 0)) for width in (OWN, OWN, D)),
    )(nb, nm, w)
    return nb.T, nm.T, w.T


def solution(mesh):
    return jax.shard_map(
        body,
        mesh=mesh,
        in_specs=(
            P("replica", "fsdp", None),
            P("replica", "fsdp"),
            P("replica", None, "fsdp"),
            P("replica", "fsdp"),
            P("replica", "fsdp"),
        ),
        out_specs=(P("replica", "fsdp"), P("replica", "fsdp"), P(None, "fsdp")),
        check_vma=False,
    )
```

```python
import jax
import jax.numpy as jnp
from jax import lax
from jax.experimental import pallas as pl
from jax.experimental.pallas import tpu as pltpu
from jax.sharding import PartitionSpec as P

D = 4096
BLOCK = 128
DOCS = 16
STEPS = 8
SIDE = 4
TOK = 128
TOK_G = 4096
COLS = 448
HALF = D // 2
OWN = D // 4
SWAP = 1024
PART = COLS // 2
TILES = 2 * STEPS
UNITS = 4 * STEPS
PASS = 1
FWD = 3
DIRECT = 1
STORES = 2
SHIP = UNITS - TILES + 2
AHEAD = 3
RELAYED = STEPS - 1

inner_rate = 2.0
outer_rate = 0.7
nesterov_coef = 0.9
epsilon = 1e-06
MESH = pl.DeviceIdType.MESH


def kernel(
    seg_ref, inp_ref, cot_ref, base_ref, mom_ref,
    nb_out, nm_out, w_out,
    xg, ysend, raw, cot, base, mom, acc, keep, xs, xr, ps, rr, wt, seg_row, seg_own, segs, weight,
    load_sem, in_sem, seg_send, seg_recv,
    a1s, a1r, a2s, a2r, a3s, a3r, b1s, b1r, b2s, b2r, b3s, b3r, ys, yr, cots, cotr, rawr, fwds,
    xss, xsr, pss, psr, wcs, wcr, wls, wlr, wfs, wfr, out_sem,
):
    rep, f = lax.axis_index("replica"), lax.axis_index("fsdp")
    lo, core = rep // 2, rep % 2
    z, x, h = f // 8, (f // 2) % 4, f % 2

    def dev(x_=x, z_=z, h_=h, lo_=lo, core_=core):
        return (lo_ * 2 + core_, z_ * 8 + x_ * 2 + h_)

    def rot(v, d):
        return lax.rem(v + d, SIDE)

    other_core = dev(core_=1 - core)
    other_lo = dev(lo_=1 - lo)
    other_h = dev(h_=1 - h)
    across = dev(h_=1 - h, lo_=1 - lo)
    at_home = (h + core) % 2 == 0
    helper = dev(h_=jnp.where(at_home, 1 - h, h), lo_=1 - lo)
    other_both = dev(lo_=1 - lo, core_=1 - core)
    along_x = [dev(x_=rot(x, d)) for d in (1, 2, 3)]
    along_z = [dev(z_=rot(z, d)) for d in (1, 2, 3)]

    def remote(src, dst, ss, rs, to):
        return pltpu.make_async_remote_copy(
            src_ref=src, dst_ref=dst, send_sem=ss, recv_sem=rs, device_id=to, device_id_type=MESH
        )

    def lanes(at, size=BLOCK):
        return pl.ds(pl.multiple_of(at, BLOCK), size)

    barrier = pltpu.get_barrier_semaphore()
    partners = along_x + along_z + [other_core, other_lo, other_h, across, other_both]
    for to in partners:
        pl.semaphore_signal(barrier, inc=1, device_id=to, device_id_type=MESH)

    load_seg = pltpu.make_async_copy(seg_ref, seg_row, load_sem.at[4])
    load_seg.start()

    def load_rows(s, part, half, stay=False):
        hh = lo if half == 0 else 1 - lo
        dst = xg.at[s, z, x, h] if stay else ysend.at[half, s]
        return pltpu.make_async_copy(
            inp_ref.at[:, lanes(hh * HALF + part * OWN + s * BLOCK)],
            dst.at[:, part * BLOCK : (part + 1) * BLOCK],
            in_sem.at[s, part, half],
        )

    def load_all(s, carry):
        for part in (0, 1):
            load_rows(s, part, 0).start()

            @pl.when(at_home)
            def _():
                load_rows(s, part, 1, True).start()

            @pl.when(jnp.logical_not(at_home))
            def _():
                load_rows(s, part, 1).start()

        return carry

    lax.fori_loop(0, STEPS, load_all, 0)
    def load_cot(u):
        return pltpu.make_async_copy(cot_ref.at[u * PART : (u + 1) * PART], raw.at[u], load_sem.at[2 + u])

    load_base = pltpu.make_async_copy(base_ref, base, load_sem.at[0])
    load_mom = pltpu.make_async_copy(mom_ref, mom, load_sem.at[1])
    load_seg.wait()
    seg_own[...] = jnp.broadcast_to(seg_row[...], (8, TOK))

    @pl.when(at_home)
    def _():
        segs[z, x, h] = jnp.broadcast_to(seg_row[...], (8, TOK))

    pl.semaphore_wait(barrier, len(partners))

    far = jnp.where(at_home, 0, 1)

    def seg_help(kind):
        return remote(seg_own, segs.at[z, x, h], seg_send.at[2, 0], seg_recv.at[2, kind], helper)

    seg_native = remote(seg_own, segs.at[z, x, h], seg_send.at[2, 1], seg_recv.at[2, 0], other_h)

    def seg_x(d):
        return remote(segs.at[z, x], segs.at[z, x], seg_send.at[0, d], seg_recv.at[0, d], along_x[d])

    def seg_z(d):
        return remote(segs.at[z], segs.at[z], seg_send.at[1, d], seg_recv.at[1, d], along_z[d])

    def cross_help(s, kind):
        return remote(ysend.at[0, s], xg.at[s, z, x, h], ys.at[0], yr.at[s, kind], helper)

    def cross_native(s):
        return remote(ysend.at[1, s], xg.at[s, z, x, h], ys.at[1], yr.at[s, 0], other_h)

    def a1(s, d):
        ref = xg.at[s, z, x, h]
        return remote(ref, ref, a1s, a1r.at[s, d], along_x[d])

    def a2(s, d):
        ref = xg.at[s, z, :, h]
        return remote(ref, ref, a2s, a2r.at[s, d], along_z[2 * d])

    def a3(s, d):
        ref = xg.at[s, rot(z, 3 - 2 * d), 2 * d : 2 * d + 2, h]
        return remote(ref, ref, a3s, a3r.at[s, d], along_z[2 * d])

    def a_far(s):
        ref = xg.at[s, z, :, h]
        return remote(ref, ref, a3s, a3r.at[s, 0], along_z[1])

    def b_far(s):
        ref = xg.at[s, :, x, 1 - h]
        return remote(ref, ref, b3s, b3r.at[s, 0], along_x[1])

    def b1(s, d):
        ref = xg.at[s, z, x, 1 - h]
        return remote(ref, ref, b1s, b1r.at[s, d], along_z[d])

    def b2(s, d):
        ref = xg.at[s, :, x, 1 - h]
        return remote(ref, ref, b2s, b2r.at[s, d], along_x[2 * d])

    def b3(s, d):
        ref = xg.at[s, 2 * d : 2 * d + 2, rot(x, 3 - 2 * d), 1 - h]
        return remote(ref, ref, b3s, b3r.at[s, d], along_x[2 * d])

    def away(body):
        pl.when(jnp.logical_not(at_home))(body)

    seg_help(far).start()
    away(lambda: seg_native.start())

    def first(s, carry):
        for part in (0, 1):
            load_rows(s, part, 0).wait()
        cross_help(s, far).start()

        @pl.when(jnp.logical_not(at_home))
        def _():
            for part in (0, 1):
                load_rows(s, part, 1).wait()
            cross_native(s).start()

        return carry

    def start_own(s):
        @pl.when(at_home)
        def _():
            for part in (0, 1):
                load_rows(s, part, 1, True).wait()

        @pl.when(jnp.logical_not(at_home))
        def _():
            cross_help(s, 1).wait_recv()

        for d in range(3):
            a1(s, d).start()

    def partner1(s):
        cross_help(s, 0).wait_recv()
        for d in range(3):
            b1(s, d).start()

    def tick(i):
        def at(s, body, end=STEPS):
            @pl.when((s >= 0) & (s < end))
            def _():
                body(s)

        def own2(s):
            for d in range(3):
                a1(s, d).wait_recv()
            for d in range(2):
                a2(s, d).start()

            @pl.when(s >= RELAYED)
            def _():
                a_far(s).start()

        def own3(s):
            for d in range(2):
                a2(s, d).wait_recv()
            for d in range(2):
                a3(s, d).start()

        def partner2(s):
            for d in range(3):
                b1(s, d).wait_recv()
            for d in range(2):
                b2(s, d).start()

            @pl.when(s >= RELAYED)
            def _():
                b_far(s).start()

        def partner3(s):
            for d in range(2):
                b2(s, d).wait_recv()
            for d in range(2):
                b3(s, d).start()

        at(i - 2, own3, RELAYED)
        at(i - 2, partner3, RELAYED)
        at(i - 1, own2)
        at(i - 1, partner2)
        at(i + 1, partner1)
        at(i + 3, start_own)

    def send_cot(u):
        @pl.when(at_home)
        def _():
            def go(i, carry):
                at = lanes(i * SWAP, SWAP)
                remote(cot_ref.at[u * PART : (u + 1) * PART, at], cot.at[2 + u, :, at], cots.at[u], cotr.at[u], across).start()
                return carry

            lax.fori_loop(0, TOK_G // SWAP, go, 0)

        @pl.when(jnp.logical_not(at_home))
        def _():
            def go(i, carry):
                at = lanes(i * SWAP, SWAP)
                remote(cot_ref.at[u * PART : (u + 1) * PART, at], raw.at[u, :, at], cots.at[u], rawr.at[u, i], other_lo).start()
                return carry

            lax.fori_loop(0, TOK_G // SWAP, go, 0)

    def pass_cot(u, first, last):
        @pl.when(jnp.logical_not(at_home))
        def _():
            def go(i, carry):
                at = lanes(i * SWAP, SWAP)
                remote(raw.at[u, :, at], raw.at[u, :, at], cots.at[u], rawr.at[u, i], other_lo).wait_recv()
                remote(raw.at[u, :, at], cot.at[2 + u, :, at], fwds.at[u], cotr.at[u], across).start()
                return carry

            lax.fori_loop(first, last, go, 0)

    lax.fori_loop(0, STEPS, first, 0)
    send_cot(0)
    send_cot(1)
    start_own(0)
    partner1(0)
    start_own(1)
    start_own(2)
    seg_help(0).wait_recv()
    away(lambda: seg_help(1).wait_recv())
    for d in range(3):
        seg_x(d).start()
    tick(0)

    @pl.when(at_home)
    def _():
        load_cot(0).start()
        load_cot(1).start()

    load_base.start()
    load_mom.start()
    for d in range(3):
        seg_x(d).wait_recv()
    for d in range(3):
        seg_z(d).start()
    tick(1)
    tick(2)
    for d in range(3):
        seg_z(d).wait_recv()
    pass_cot(0, 0, 2)
    tick(3)
    pass_cot(0, 2, TOK_G // SWAP)

    ids = segs[...].reshape(TOK_G // TOK, 8, TOK)
    per_token = jnp.zeros((TOK_G // TOK, 8, TOK), jnp.float32)
    for doc in range(DOCS):
        mine = (ids == doc).astype(jnp.float32)
        count = jnp.sum(jnp.sum(mine, axis=0), axis=1, keepdims=True)
        per_token = per_token + mine * (1.0 / count)[None]
    weight[...] = per_token

    def scale_cot(src, g):
        def tile(i, carry):
            at = lanes(i * TOK)
            block = src[:, at].astype(jnp.float32).reshape(PART // 8, 8, TOK)
            cot[g, :, at] = (block * weight[i][None]).reshape(PART, TOK).astype(jnp.bfloat16)
            return carry

        lax.fori_loop(0, TOK_G // TOK, tile, 0)

    def scale_own(u):
        @pl.when(at_home)
        def _():
            load_cot(u).wait()

        scale_cot(raw.at[u], u)

    scale_own(0)

    def swap(j):
        return remote(xs.at[j], xr.at[j], xss, xsr.at[j], other_core)

    def to_owner(j, g, s):
        k, side = (g % 2) * STEPS + s, g // 2
        return remote(ps.at[j], rr.at[k, side], pss, psr.at[k, side], dev(h_=jnp.where(g < 2, h, 1 - h), lo_=1 - lo))

    def from_owner(k, side):
        return remote(ps.at[0], rr.at[k, side], pss, psr.at[k, side], other_lo)

    def place(k, ref, rp=None):
        u, s = k // STEPS, k % STEPS
        first = s * BLOCK if rp is None else rp * OWN + s * BLOCK
        return ref.at[pl.ds(pl.multiple_of(u * PART, 32), PART), lanes(first)]

    def w_core(k):
        return remote(wt.at[k], place(k, w_out, rep), wcs, wcr, other_core)

    def w_lo(k):
        return remote(wt.at[k], place(k, w_out, rep), wls, wlr.at[k], other_lo)

    def w_fwd(k):
        there = place(k, w_out, (1 - lo) * 2 + core)
        return remote(there, there, wfs, wfr, other_core)

    def w_diag(k):
        return remote(wt.at[k], place(k, w_out, rep), wfs, wfr, other_both)

    def w_own(k):
        return pltpu.make_async_copy(wt.at[k], place(k, w_out, rep), out_sem.at[0])

    def nm_own(k):
        return pltpu.make_async_copy(place(k, mom), place(k, nm_out), out_sem.at[1])

    def nb_own(k):
        return pltpu.make_async_copy(place(k, base), place(k, nb_out), out_sem.at[2])

    def quantized(at):
        blk = inner_rate * acc[:, lanes(at * BLOCK)]
        scale = (jnp.max(jnp.abs(blk), axis=1, keepdims=True) + epsilon).astype(jnp.bfloat16)
        scale = scale.astype(jnp.float32)
        coded = (blk * (1.0 / scale)).astype(jnp.bfloat16)
        return coded.astype(jnp.float32) * scale

    def pick(j, *cases):
        value = cases[-1]
        for bound, case in reversed(cases[:-1]):
            value = jnp.where(j < bound, case, value)
        return value

    def unit(j):
        g = pick(j, (6, j // 3), (10, j % 2), (15, 2), (21, j % 3), (28, 3), (31, j - 28), 3)
        s = pick(j, (6, j % 3), (10, j // 2), (15, j - 10), (21, j // 3), (28, j - 21), STEPS - 1)
        return g, s

    def tile_of(m):
        return pick(m, (7, m), (14, m + 1), (15, 7), m)

    def step(j, carry):
        @pl.when(j < UNITS)
        def _():
            g, s = unit(j)

            @pl.when(g == 0)
            def _():
                @pl.when(s < RELAYED)
                def _():
                    for d in range(2):
                        a3(s, d).wait_recv()
                        b3(s, d).wait_recv()

                @pl.when(s >= RELAYED)
                def _():
                    for d in range(2):
                        a2(s, d).wait_recv()
                        b2(s, d).wait_recv()
                    a_far(s).wait_recv()
                    b_far(s).wait_recv()

            @pl.when(j == 3)
            def _():
                pass_cot(1, 0, TOK_G // SWAP)
                scale_own(1)

            for u, at in ((0, 10), (1, 21)):

                @pl.when(j == at)
                def _():
                    got = cot.at[2 + u]
                    pltpu.make_async_copy(got, got, cotr.at[u]).wait()
                    scale_cot(got, 2 + u)

            acc[...] = jnp.dot(cot[g], xg[s].reshape(TOK_G, 2 * BLOCK), preferred_element_type=jnp.float32)
            xs[j] = quantized(1 - core)
            swap(j).start()
            keep[j % 4] = quantized(core)

            @pl.when(((g == 0) & (s > 0) & (s < 3)) | ((g == 1) & (s >= 3)))
            def _():
                tick(s + AHEAD)

        @pl.when((j >= PASS) & (j < UNITS + PASS))
        def _():
            q = j - PASS
            g, s = unit(q)
            swap(q).wait_recv()
            ps[q] = (keep[q % 4] + xr[q]).astype(jnp.bfloat16)
            to_owner(q, g, s).start()

        @pl.when(j == SHIP)
        def _():
            load_base.wait()
            load_mom.wait()

        @pl.when((j >= SHIP) & (j < SHIP + TILES))
        def _():
            k = tile_of(j - SHIP)
            from_owner(k, 0).wait_recv()
            from_owner(k, 1).wait_recv()
            average = (rr[k, 0].astype(jnp.float32) + rr[k, 1].astype(jnp.float32)) * 0.25
            u, s = k // STEPS, k % STEPS
            cols, at = pl.ds(pl.multiple_of(u * PART, 32), PART), lanes(s * BLOCK)
            nm = nesterov_coef * mom[cols, at] + average
            nb = base[cols, at] - outer_rate * (average + nesterov_coef * nm)
            wt[k] = nb.astype(jnp.bfloat16)
            w_lo(k).start()

            @pl.when(j >= SHIP + TILES - DIRECT)
            def _():
                w_diag(k).start()

            w_core(k).start()
            mom[cols, at] = nm
            base[cols, at] = nb
            w_own(k).start()
            nm_own(k).start()
            nb_own(k).start()

        @pl.when((j >= SHIP + FWD) & (j < SHIP + FWD + TILES - DIRECT))
        def _():
            k = tile_of(j - (SHIP + FWD))
            w_lo(k).wait_recv()
            w_fwd(k).start()

        return carry

    lax.fori_loop(0, SHIP + TILES + max(0, FWD - DIRECT), step, 0)

    for d in range(3):
        seg_x(d).wait_send()
        seg_z(d).wait_send()
    seg_help(far).wait_send()
    away(lambda: seg_native.wait_send())

    def drain(ref, sem):
        pltpu.make_async_copy(ref, ref, sem).wait()

    for sem in (a1s, b1s):
        drain(xg.at[0, :3], sem)
    for sem in (a2s, b2s):
        drain(xg.at[:2], sem)
    for sem in (a3s, b3s):
        drain(xg.at[:1], sem)
    drain(ysend.at[0], ys.at[0])
    away(lambda: drain(ysend.at[1], ys.at[1]))
    drain(xs, xss)
    drain(ps, pss)
    for u in (0, 1):
        pltpu.make_async_copy(cot.at[2 + u], cot.at[2 + u], cots.at[u]).wait()

        @pl.when(jnp.logical_not(at_home))
        def _():
            pltpu.make_async_copy(cot.at[2 + u], cot.at[2 + u], fwds.at[u]).wait()

    for sem in (wcs, wls, wfs, wcr, wfr, out_sem.at[0]):
        drain(wt, sem)
    for m in range(TILES - DIRECT, TILES):
        w_lo(tile_of(m)).wait_recv()
    drain(mom, out_sem.at[1])
    drain(base, out_sem.at[2])


def store(nb, nm, w, nb_out, nm_out, w_out):
    nb_out[...] = nb[...]
    nm_out[...] = nm[...]
    w_out[...] = w[...]


def body(inputs, segments, cotangent, base, momentum):
    bf, f32, dma = jnp.bfloat16, jnp.float32, pltpu.SemaphoreType.DMA
    hbm = pl.BlockSpec(memory_space=pl.ANY)
    nb, nm, w = pl.pallas_call(
        kernel,
        out_shape=(
            jax.ShapeDtypeStruct((COLS, OWN), f32),
            jax.ShapeDtypeStruct((COLS, OWN), f32),
            jax.ShapeDtypeStruct((COLS, D), bf),
        ),
        in_specs=[hbm] * 5,
        out_specs=(hbm, hbm, hbm),
        scratch_shapes=[
            pltpu.VMEM((STEPS, SIDE, SIDE, 2, TOK, 2 * BLOCK), bf),
            pltpu.VMEM((2, STEPS, TOK, 2 * BLOCK), bf),
            pltpu.VMEM((2, PART, TOK_G), bf),
            pltpu.VMEM((4, PART, TOK_G), bf),
            pltpu.VMEM((COLS, OWN), f32),
            pltpu.VMEM((COLS, OWN), f32),
            pltpu.VMEM((PART, 2 * BLOCK), f32),
            pltpu.VMEM((4, PART, BLOCK), f32),
            pltpu.VMEM((UNITS, PART, BLOCK), f32),
            pltpu.VMEM((UNITS, PART, BLOCK), f32),
            pltpu.VMEM((UNITS, PART, BLOCK), bf),
            pltpu.VMEM((TILES, 2, PART, BLOCK), bf),
            pltpu.VMEM((TILES, PART, BLOCK), bf),
            pltpu.VMEM((1, TOK), jnp.int32),
            pltpu.VMEM((8, TOK), jnp.int32),
            pltpu.VMEM((SIDE, SIDE, 2, 8, TOK), jnp.int32),
            pltpu.VMEM((TOK_G // TOK, 8, TOK), f32),
            dma((5,)), dma((STEPS, 2, 2)), dma((3, 3)), dma((3, 3)),
            dma, dma((STEPS, 3)), dma, dma((STEPS, 2)), dma, dma((STEPS, 2)),
            dma, dma((STEPS, 3)), dma, dma((STEPS, 2)), dma, dma((STEPS, 2)),
            dma((2,)), dma((STEPS, 2)), dma((2,)), dma((2,)), dma((2, TOK_G // SWAP)), dma((2,)),
            dma, dma((UNITS,)), dma, dma((TILES, 2)),
            dma, dma, dma, dma((TILES,)), dma, dma, dma((3,)),
        ],
        compiler_params=pltpu.CompilerParams(
            collective_id=0, has_side_effects=True, vmem_limit_bytes=60 * 2**20
        ),
        cost_estimate=pl.CostEstimate(flops=2 * D * D * COLS, bytes_accessed=2**24, transcendentals=0),
    )(segments, inputs[0], cotangent[0].T, base.T, momentum.T)
    nb, nm, w = pl.pallas_call(
        store,
        out_shape=(
            jax.ShapeDtypeStruct((COLS, OWN), f32),
            jax.ShapeDtypeStruct((COLS, OWN), f32),
            jax.ShapeDtypeStruct((COLS, D), bf),
        ),
        compiler_params=pltpu.CompilerParams(vmem_limit_bytes=60 * 2**20),
        grid=(STORES,),
        in_specs=[pl.BlockSpec((COLS // STORES, width), lambda i: (i, 0)) for width in (OWN, OWN, D)],
        out_specs=tuple(pl.BlockSpec((COLS // STORES, width), lambda i: (i, 0)) for width in (OWN, OWN, D)),
    )(nb, nm, w)
    return nb.T, nm.T, w.T


def solution(mesh):
    return jax.shard_map(
        body,
        mesh=mesh,
        in_specs=(
            P("replica", "fsdp", None),
            P("replica", "fsdp"),
            P("replica", None, "fsdp"),
            P("replica", "fsdp"),
            P("replica", "fsdp"),
        ),
        out_specs=(P("replica", "fsdp"), P("replica", "fsdp"), P(None, "fsdp")),
        check_vma=False,
    )
```

```python
import jax
import jax.numpy as jnp
from jax import lax
from jax.experimental import pallas as pl
from jax.experimental.pallas import tpu as pltpu
from jax.sharding import PartitionSpec as P

D = 4096
BLOCK = 128
DOCS = 16
STEPS = 8
SIDE = 4
TOK = 128
TOK_G = 4096
COLS = 448
HALF = D // 2
OWN = D // 4
SWAP = 1024
PART = COLS // 2
TILES = 2 * STEPS
UNITS = 4 * STEPS
PASS = 1
FWD = 3
DIRECT = 1
STORES = 2
SHIP = UNITS - TILES + 2
AHEAD = 3
RELAYED = STEPS - 1

inner_rate = 2.0
outer_rate = 0.7
nesterov_coef = 0.9
epsilon = 1e-06
MESH = pl.DeviceIdType.MESH


def kernel(
    seg_ref, inp_ref, cot_ref, base_ref, mom_ref,
    nb_out, nm_out, w_out,
    xg, ysend, raw, cot, base, mom, acc, keep, xs, xr, ps, rr, wt, seg_row, seg_own, segs, weight,
    load_sem, in_sem, seg_send, seg_recv,
    a1s, a1r, a2s, a2r, a3s, a3r, b1s, b1r, b2s, b2r, b3s, b3r, ys, yr, cots, cotr, rawr, fwds,
    xss, xsr, pss, psr, wcs, wcr, wls, wlr, wfs, wfr, out_sem,
):
    rep, f = lax.axis_index("replica"), lax.axis_index("fsdp")
    lo, core = rep // 2, rep % 2
    z, x, h = f // 8, (f // 2) % 4, f % 2

    def dev(x_=x, z_=z, h_=h, lo_=lo, core_=core):
        return (lo_ * 2 + core_, z_ * 8 + x_ * 2 + h_)

    def rot(v, d):
        return lax.rem(v + d, SIDE)

    other_core = dev(core_=1 - core)
    other_lo = dev(lo_=1 - lo)
    other_h = dev(h_=1 - h)
    across = dev(h_=1 - h, lo_=1 - lo)
    at_home = (h + core) % 2 == 0
    helper = dev(h_=jnp.where(at_home, 1 - h, h), lo_=1 - lo)
    other_both = dev(lo_=1 - lo, core_=1 - core)
    along_x = [dev(x_=rot(x, d)) for d in (1, 2, 3)]
    along_z = [dev(z_=rot(z, d)) for d in (1, 2, 3)]

    def remote(src, dst, ss, rs, to):
        return pltpu.make_async_remote_copy(
            src_ref=src, dst_ref=dst, send_sem=ss, recv_sem=rs, device_id=to, device_id_type=MESH
        )

    def lanes(at, size=BLOCK):
        return pl.ds(pl.multiple_of(at, BLOCK), size)

    barrier = pltpu.get_barrier_semaphore()
    partners = along_x + along_z + [other_core, other_lo, other_h, across, other_both]
    for to in partners:
        pl.semaphore_signal(barrier, inc=1, device_id=to, device_id_type=MESH)

    load_seg = pltpu.make_async_copy(seg_ref, seg_row, load_sem.at[4])
    load_seg.start()

    def load_rows(s, part, half, stay=False):
        hh = lo if half == 0 else 1 - lo
        dst = xg.at[s, z, x, h] if stay else ysend.at[half, s]
        return pltpu.make_async_copy(
            inp_ref.at[:, lanes(hh * HALF + part * OWN + s * BLOCK)],
            dst.at[:, part * BLOCK : (part + 1) * BLOCK],
            in_sem.at[s, part, half],
        )

    def load_all(s, carry):
        for part in (0, 1):
            load_rows(s, part, 0).start()

            @pl.when(at_home)
            def _():
                load_rows(s, part, 1, True).start()

            @pl.when(jnp.logical_not(at_home))
            def _():
                load_rows(s, part, 1).start()

        return carry

    lax.fori_loop(0, STEPS, load_all, 0)
    def load_cot(u):
        return pltpu.make_async_copy(cot_ref.at[u * PART : (u + 1) * PART], raw.at[u], load_sem.at[2 + u])

    load_base = pltpu.make_async_copy(base_ref, base, load_sem.at[0])
    load_mom = pltpu.make_async_copy(mom_ref, mom, load_sem.at[1])
    load_seg.wait()
    seg_own[...] = jnp.broadcast_to(seg_row[...], (8, TOK))

    @pl.when(at_home)
    def _():
        segs[z, x, h] = jnp.broadcast_to(seg_row[...], (8, TOK))

    pl.semaphore_wait(barrier, len(partners))

    far = jnp.where(at_home, 0, 1)

    def seg_help(kind):
        return remote(seg_own, segs.at[z, x, h], seg_send.at[2, 0], seg_recv.at[2, kind], helper)

    seg_native = remote(seg_own, segs.at[z, x, h], seg_send.at[2, 1], seg_recv.at[2, 0], other_h)

    def seg_x(d):
        return remote(segs.at[z, x], segs.at[z, x], seg_send.at[0, d], seg_recv.at[0, d], along_x[d])

    def seg_z(d):
        return remote(segs.at[z], segs.at[z], seg_send.at[1, d], seg_recv.at[1, d], along_z[d])

    def cross_help(s, kind):
        return remote(ysend.at[0, s], xg.at[s, z, x, h], ys.at[0], yr.at[s, kind], helper)

    def cross_native(s):
        return remote(ysend.at[1, s], xg.at[s, z, x, h], ys.at[1], yr.at[s, 0], other_h)

    def a1(s, d):
        ref = xg.at[s, z, x, h]
        return remote(ref, ref, a1s, a1r.at[s, d], along_x[d])

    def a2(s, d):
        ref = xg.at[s, z, :, h]
        return remote(ref, ref, a2s, a2r.at[s, d], along_z[2 * d])

    def a3(s, d):
        ref = xg.at[s, rot(z, 3 - 2 * d), 2 * d : 2 * d + 2, h]
        return remote(ref, ref, a3s, a3r.at[s, d], along_z[2 * d])

    def a_far(s):
        ref = xg.at[s, z, :, h]
        return remote(ref, ref, a3s, a3r.at[s, 0], along_z[1])

    def b_far(s):
        ref = xg.at[s, :, x, 1 - h]
        return remote(ref, ref, b3s, b3r.at[s, 0], along_x[1])

    def b1(s, d):
        ref = xg.at[s, z, x, 1 - h]
        return remote(ref, ref, b1s, b1r.at[s, d], along_z[d])

    def b2(s, d):
        ref = xg.at[s, :, x, 1 - h]
        return remote(ref, ref, b2s, b2r.at[s, d], along_x[2 * d])

    def b3(s, d):
        ref = xg.at[s, 2 * d : 2 * d + 2, rot(x, 3 - 2 * d), 1 - h]
        return remote(ref, ref, b3s, b3r.at[s, d], along_x[2 * d])

    def away(body):
        pl.when(jnp.logical_not(at_home))(body)

    seg_help(far).start()
    away(lambda: seg_native.start())

    def first(s, carry):
        for part in (0, 1):
            load_rows(s, part, 0).wait()
        cross_help(s, far).start()

        @pl.when(jnp.logical_not(at_home))
        def _():
            for part in (0, 1):
                load_rows(s, part, 1).wait()
            cross_native(s).start()

        return carry

    def start_own(s):
        @pl.when(at_home)
        def _():
            for part in (0, 1):
                load_rows(s, part, 1, True).wait()

        @pl.when(jnp.logical_not(at_home))
        def _():
            cross_help(s, 1).wait_recv()

        for d in range(3):
            a1(s, d).start()

    def partner1(s):
        cross_help(s, 0).wait_recv()
        for d in range(3):
            b1(s, d).start()

    def tick(i):
        def at(s, body, end=STEPS):
            @pl.when((s >= 0) & (s < end))
            def _():
                body(s)

        def own2(s):
            for d in range(3):
                a1(s, d).wait_recv()
            for d in range(2):
                a2(s, d).start()

            @pl.when(s >= RELAYED)
            def _():
                a_far(s).start()

        def own3(s):
            for d in range(2):
                a2(s, d).wait_recv()
            for d in range(2):
                a3(s, d).start()

        def partner2(s):
            for d in range(3):
                b1(s, d).wait_recv()
            for d in range(2):
                b2(s, d).start()

            @pl.when(s >= RELAYED)
            def _():
                b_far(s).start()

        def partner3(s):
            for d in range(2):
                b2(s, d).wait_recv()
            for d in range(2):
                b3(s, d).start()

        at(i - 2, own3, RELAYED)
        at(i - 2, partner3, RELAYED)
        at(i - 1, own2)
        at(i - 1, partner2)
        at(i + 1, partner1)
        at(i + 3, start_own)

    def send_cot(u):
        @pl.when(at_home)
        def _():
            def go(i, carry):
                at = lanes(i * SWAP, SWAP)
                remote(cot_ref.at[u * PART : (u + 1) * PART, at], cot.at[2 + u, :, at], cots.at[u], cotr.at[u], across).start()
                return carry

            lax.fori_loop(0, TOK_G // SWAP, go, 0)

        @pl.when(jnp.logical_not(at_home))
        def _():
            def go(i, carry):
                at = lanes(i * SWAP, SWAP)
                remote(cot_ref.at[u * PART : (u + 1) * PART, at], raw.at[u, :, at], cots.at[u], rawr.at[u, i], other_lo).start()
                return carry

            lax.fori_loop(0, TOK_G // SWAP, go, 0)

    def pass_cot(u, first, last):
        @pl.when(jnp.logical_not(at_home))
        def _():
            def go(i, carry):
                at = lanes(i * SWAP, SWAP)
                remote(raw.at[u, :, at], raw.at[u, :, at], cots.at[u], rawr.at[u, i], other_lo).wait_recv()
                remote(raw.at[u, :, at], cot.at[2 + u, :, at], fwds.at[u], cotr.at[u], across).start()
                return carry

            lax.fori_loop(first, last, go, 0)

    lax.fori_loop(0, STEPS, first, 0)
    send_cot(0)
    send_cot(1)
    start_own(0)
    partner1(0)
    start_own(1)
    start_own(2)
    seg_help(0).wait_recv()
    away(lambda: seg_help(1).wait_recv())
    for d in range(3):
        seg_x(d).start()
    tick(0)

    @pl.when(at_home)
    def _():
        load_cot(0).start()
        load_cot(1).start()

    load_base.start()
    load_mom.start()
    for d in range(3):
        seg_x(d).wait_recv()
    for d in range(3):
        seg_z(d).start()
    tick(1)
    tick(2)
    for d in range(3):
        seg_z(d).wait_recv()
    pass_cot(0, 0, 2)
    tick(3)
    pass_cot(0, 2, TOK_G // SWAP)

    ids = segs[...].reshape(TOK_G // TOK, 8, TOK)
    per_token = jnp.zeros((TOK_G // TOK, 8, TOK), jnp.float32)
    for doc in range(DOCS):
        mine = (ids == doc).astype(jnp.float32)
        count = jnp.sum(jnp.sum(mine, axis=0), axis=1, keepdims=True)
        per_token = per_token + mine * (1.0 / count)[None]
    weight[...] = per_token

    def scale_cot(src, g):
        def tile(i, carry):
            at = lanes(i * TOK)
            block = src[:, at].astype(jnp.float32).reshape(PART // 8, 8, TOK)
            cot[g, :, at] = (block * weight[i][None]).reshape(PART, TOK).astype(jnp.bfloat16)
            return carry

        lax.fori_loop(0, TOK_G // TOK, tile, 0, unroll=4)

    def scale_own(u):
        @pl.when(at_home)
        def _():
            load_cot(u).wait()

        scale_cot(raw.at[u], u)

    scale_own(0)

    def swap(j):
        return remote(xs.at[j], xr.at[j], xss, xsr.at[j], other_core)

    def to_owner(j, g, s):
        k, side = (g % 2) * STEPS + s, g // 2
        return remote(ps.at[j], rr.at[k, side], pss, psr.at[k, side], dev(h_=jnp.where(g < 2, h, 1 - h), lo_=1 - lo))

    def from_owner(k, side):
        return remote(ps.at[0], rr.at[k, side], pss, psr.at[k, side], other_lo)

    def place(k, ref, rp=None):
        u, s = k // STEPS, k % STEPS
        first = s * BLOCK if rp is None else rp * OWN + s * BLOCK
        return ref.at[pl.ds(pl.multiple_of(u * PART, 32), PART), lanes(first)]

    def w_core(k):
        return remote(wt.at[k], place(k, w_out, rep), wcs, wcr, other_core)

    def w_lo(k):
        return remote(wt.at[k], place(k, w_out, rep), wls, wlr.at[k], other_lo)

    def w_fwd(k):
        there = place(k, w_out, (1 - lo) * 2 + core)
        return remote(there, there, wfs, wfr, other_core)

    def w_diag(k):
        return remote(wt.at[k], place(k, w_out, rep), wfs, wfr, other_both)

    def w_own(k):
        return pltpu.make_async_copy(wt.at[k], place(k, w_out, rep), out_sem.at[0])

    def nm_own(k):
        return pltpu.make_async_copy(place(k, mom), place(k, nm_out), out_sem.at[1])

    def nb_own(k):
        return pltpu.make_async_copy(place(k, base), place(k, nb_out), out_sem.at[2])

    def quantized(at):
        blk = inner_rate * acc[:, lanes(at * BLOCK)]
        scale = (jnp.max(jnp.abs(blk), axis=1, keepdims=True) + epsilon).astype(jnp.bfloat16)
        scale = scale.astype(jnp.float32)
        coded = (blk * (1.0 / scale)).astype(jnp.bfloat16)
        return coded.astype(jnp.float32) * scale

    def pick(j, *cases):
        value = cases[-1]
        for bound, case in reversed(cases[:-1]):
            value = jnp.where(j < bound, case, value)
        return value

    def unit(j):
        g = pick(j, (6, j // 3), (10, j % 2), (15, 2), (21, j % 3), (28, 3), (31, j - 28), 3)
        s = pick(j, (6, j % 3), (10, j // 2), (15, j - 10), (21, j // 3), (28, j - 21), STEPS - 1)
        return g, s

    def tile_of(m):
        return pick(m, (7, m), (14, m + 1), (15, 7), m)

    def step(j, carry):
        @pl.when(j < UNITS)
        def _():
            g, s = unit(j)

            @pl.when(g == 0)
            def _():
                @pl.when(s < RELAYED)
                def _():
                    for d in range(2):
                        a3(s, d).wait_recv()
                        b3(s, d).wait_recv()

                @pl.when(s >= RELAYED)
                def _():
                    for d in range(2):
                        a2(s, d).wait_recv()
                        b2(s, d).wait_recv()
                    a_far(s).wait_recv()
                    b_far(s).wait_recv()

            @pl.when(j == 3)
            def _():
                pass_cot(1, 0, TOK_G // SWAP)
                scale_own(1)

            for u, at in ((0, 10), (1, 21)):

                @pl.when(j == at)
                def _():
                    got = cot.at[2 + u]
                    pltpu.make_async_copy(got, got, cotr.at[u]).wait()
                    scale_cot(got, 2 + u)

            acc[...] = jnp.dot(cot[g], xg[s].reshape(TOK_G, 2 * BLOCK), preferred_element_type=jnp.float32)
            xs[j] = quantized(1 - core)
            swap(j).start()
            keep[j % 4] = quantized(core)

            @pl.when(((g == 0) & (s > 0) & (s < 3)) | ((g == 1) & (s >= 3)))
            def _():
                tick(s + AHEAD)

        @pl.when((j >= PASS) & (j < UNITS + PASS))
        def _():
            q = j - PASS
            g, s = unit(q)
            swap(q).wait_recv()
            ps[q] = (keep[q % 4] + xr[q]).astype(jnp.bfloat16)
            to_owner(q, g, s).start()

        @pl.when(j == SHIP)
        def _():
            load_base.wait()
            load_mom.wait()

        @pl.when((j >= SHIP) & (j < SHIP + TILES))
        def _():
            k = tile_of(j - SHIP)
            from_owner(k, 0).wait_recv()
            from_owner(k, 1).wait_recv()
            average = (rr[k, 0].astype(jnp.float32) + rr[k, 1].astype(jnp.float32)) * 0.25
            u, s = k // STEPS, k % STEPS
            cols, at = pl.ds(pl.multiple_of(u * PART, 32), PART), lanes(s * BLOCK)
            nm = nesterov_coef * mom[cols, at] + average
            nb = base[cols, at] - outer_rate * (average + nesterov_coef * nm)
            wt[k] = nb.astype(jnp.bfloat16)
            w_lo(k).start()

            @pl.when(j >= SHIP + TILES - DIRECT)
            def _():
                w_diag(k).start()

            w_core(k).start()
            mom[cols, at] = nm
            base[cols, at] = nb
            w_own(k).start()
            nm_own(k).start()
            nb_own(k).start()

        @pl.when((j >= SHIP + FWD) & (j < SHIP + FWD + TILES - DIRECT))
        def _():
            k = tile_of(j - (SHIP + FWD))
            w_lo(k).wait_recv()
            w_fwd(k).start()

        return carry

    lax.fori_loop(0, SHIP + TILES + max(0, FWD - DIRECT), step, 0)

    for d in range(3):
        seg_x(d).wait_send()
        seg_z(d).wait_send()
    seg_help(far).wait_send()
    away(lambda: seg_native.wait_send())

    def drain(ref, sem):
        pltpu.make_async_copy(ref, ref, sem).wait()

    for sem in (a1s, b1s):
        drain(xg.at[0, :3], sem)
    for sem in (a2s, b2s):
        drain(xg.at[:2], sem)
    for sem in (a3s, b3s):
        drain(xg.at[:1], sem)
    drain(ysend.at[0], ys.at[0])
    away(lambda: drain(ysend.at[1], ys.at[1]))
    drain(xs, xss)
    drain(ps, pss)
    for u in (0, 1):
        pltpu.make_async_copy(cot.at[2 + u], cot.at[2 + u], cots.at[u]).wait()

        @pl.when(jnp.logical_not(at_home))
        def _():
            pltpu.make_async_copy(cot.at[2 + u], cot.at[2 + u], fwds.at[u]).wait()

    for sem in (wcs, wls, wfs, wcr, wfr, out_sem.at[0]):
        drain(wt, sem)
    for m in range(TILES - DIRECT, TILES):
        w_lo(tile_of(m)).wait_recv()
    drain(mom, out_sem.at[1])
    drain(base, out_sem.at[2])


def store(nb, nm, w, nb_out, nm_out, w_out):
    nb_out[...] = nb[...]
    nm_out[...] = nm[...]
    w_out[...] = w[...]


def body(inputs, segments, cotangent, base, momentum):
    bf, f32, dma = jnp.bfloat16, jnp.float32, pltpu.SemaphoreType.DMA
    hbm = pl.BlockSpec(memory_space=pl.ANY)
    nb, nm, w = pl.pallas_call(
        kernel,
        out_shape=(
            jax.ShapeDtypeStruct((COLS, OWN), f32),
            jax.ShapeDtypeStruct((COLS, OWN), f32),
            jax.ShapeDtypeStruct((COLS, D), bf),
        ),
        in_specs=[hbm] * 5,
        out_specs=(hbm, hbm, hbm),
        scratch_shapes=[
            pltpu.VMEM((STEPS, SIDE, SIDE, 2, TOK, 2 * BLOCK), bf),
            pltpu.VMEM((2, STEPS, TOK, 2 * BLOCK), bf),
            pltpu.VMEM((2, PART, TOK_G), bf),
            pltpu.VMEM((4, PART, TOK_G), bf),
            pltpu.VMEM((COLS, OWN), f32),
            pltpu.VMEM((COLS, OWN), f32),
            pltpu.VMEM((PART, 2 * BLOCK), f32),
            pltpu.VMEM((4, PART, BLOCK), f32),
            pltpu.VMEM((UNITS, PART, BLOCK), f32),
            pltpu.VMEM((UNITS, PART, BLOCK), f32),
            pltpu.VMEM((UNITS, PART, BLOCK), bf),
            pltpu.VMEM((TILES, 2, PART, BLOCK), bf),
            pltpu.VMEM((TILES, PART, BLOCK), bf),
            pltpu.VMEM((1, TOK), jnp.int32),
            pltpu.VMEM((8, TOK), jnp.int32),
            pltpu.VMEM((SIDE, SIDE, 2, 8, TOK), jnp.int32),
            pltpu.VMEM((TOK_G // TOK, 8, TOK), f32),
            dma((5,)), dma((STEPS, 2, 2)), dma((3, 3)), dma((3, 3)),
            dma, dma((STEPS, 3)), dma, dma((STEPS, 2)), dma, dma((STEPS, 2)),
            dma, dma((STEPS, 3)), dma, dma((STEPS, 2)), dma, dma((STEPS, 2)),
            dma((2,)), dma((STEPS, 2)), dma((2,)), dma((2,)), dma((2, TOK_G // SWAP)), dma((2,)),
            dma, dma((UNITS,)), dma, dma((TILES, 2)),
            dma, dma, dma, dma((TILES,)), dma, dma, dma((3,)),
        ],
        compiler_params=pltpu.CompilerParams(
            collective_id=0, has_side_effects=True, vmem_limit_bytes=60 * 2**20
        ),
        cost_estimate=pl.CostEstimate(flops=2 * D * D * COLS, bytes_accessed=2**24, transcendentals=0),
    )(segments, inputs[0], cotangent[0].T, base.T, momentum.T)
    nb, nm, w = pl.pallas_call(
        store,
        out_shape=(
            jax.ShapeDtypeStruct((COLS, OWN), f32),
            jax.ShapeDtypeStruct((COLS, OWN), f32),
            jax.ShapeDtypeStruct((COLS, D), bf),
        ),
        compiler_params=pltpu.CompilerParams(vmem_limit_bytes=60 * 2**20),
        grid=(STORES,),
        in_specs=[pl.BlockSpec((COLS // STORES, width), lambda i: (i, 0)) for width in (OWN, OWN, D)],
        out_specs=tuple(pl.BlockSpec((COLS // STORES, width), lambda i: (i, 0)) for width in (OWN, OWN, D)),
    )(nb, nm, w)
    return nb.T, nm.T, w.T


def solution(mesh):
    return jax.shard_map(
        body,
        mesh=mesh,
        in_specs=(
            P("replica", "fsdp", None),
            P("replica", "fsdp"),
            P("replica", None, "fsdp"),
            P("replica", "fsdp"),
            P("replica", "fsdp"),
        ),
        out_specs=(P("replica", "fsdp"), P("replica", "fsdp"), P(None, "fsdp")),
        check_vma=False,
    )
```
